256 devices in a mesh: span: 32 (over z, y), deck: 8 (over x, core).
Axes of the slice: x: 4, y: 4, z: 8, core: 2. Of those that a mesh axis runs over, the one named last changes fastest.
Arguments:
- flex: float32 [32, 8, 1024, 1024], P('span', 'deck'), may hold values from -16 to 16, as said below
- precond: float32 [32, 8, 1024, 1024], P('span', 'deck'), may hold values from -16 to 16, as said below
- corner_map: float32 [32, 8, 256, 1024], P('span', 'deck'), may hold values from -0.1875 to 0.1875
- coarse_inverse: float32 [256, 256], replicated, may hold values from -16 to 16, as said below
- gap_deck: float32 [32, 8, 256, 256], P('span', 'deck'), may hold values from -6 to 6
- gap_joint: float32 [32, 8, 256, 256], P('span', 'deck'), may hold values from -6 to 6
- active: int32 [32, 8, 4], P('span', 'deck'), may hold values 0 or 1
Outputs:
- solution_deck: float32 [32, 8, 256, 256], P('span', 'deck')
- solution_joint: float32 [32, 8, 256, 256], P('span', 'deck')
- residual_deck: float32 [32, 8, 256, 256], P('span', 'deck')
- residual_joint: float32 [32, 8, 256, 256], P('span', 'deck')
The draws below stay inside these ranges and needn't reach their ends.
Inputs may be any that keep to these rules, and one draw needn't show every extreme that they name: flex is symmetric positive definite for every subdomain. precond is symmetric positive definite for every subdomain. coarse_inverse is symmetric positive definite.
All inputs are finite; a program needn't handle non-finite values. No bound on the sum of `active` on one device may be relied on, other than what follows from the above.
Results may differ from the reference program's by a relative error of at most 0.00024.
Values sent between devices are 32-bit elements; how exact they have to be, the bound alone decides.
No kernel may reach another device: no remote copies, remote signals or barrier semaphores. Data moves between devices by JAX's collectives and lax.ppermute only.
A program may use at most 64 MiB of HBM per device.

```python
import math
import jax
import jax.numpy as jnp
from jax import lax

IFACE = 1024
NC = 256
GB = 4
ITERS = 2
CASES = 256
FACE = 256
SPANS = 32
DECKS = 8


def assemble(noise, diagonal_values, order):
    symmetric = (noise + jnp.swapaxes(noise, -1, -2)) * (0.42 / math.sqrt(order))
    identity = jnp.eye(order, dtype=jnp.float32)
    matrix = symmetric * (1.0 - identity) + identity * diagonal_values[..., None, :]
    return matrix


def draw_flex(key, part):
    key = jax.random.fold_in(key, 11)
    key_noise, key_diag = jax.random.split(key, 2)
    dims_full = (SPANS, DECKS, IFACE, IFACE)
    noise = jax.random.truncated_normal(key_noise, -3.0, 3.0, dims_full, jnp.float32)
    diagonal_values = jax.random.uniform(key_diag, (SPANS, DECKS, IFACE), jnp.float32, 2.0, 4.0)
    return assemble(noise, diagonal_values, IFACE)


def draw_precond(key, part):
    key = jax.random.fold_in(key, 12)
    key_noise, key_diag = jax.random.split(key, 2)
    dims_full = (SPANS, DECKS, IFACE, IFACE)
    noise = jax.random.truncated_normal(key_noise, -3.0, 3.0, dims_full, jnp.float32)
    diagonal_values = jax.random.uniform(key_diag, (SPANS, DECKS, IFACE), jnp.float32, 1.5, 3.5)
    return assemble(noise, diagonal_values, IFACE)


def draw_coarse_inverse(key, part):
    key = jax.random.fold_in(key, 13)
    key_noise, key_diag = jax.random.split(key, 2)
    noise = jax.random.truncated_normal(key_noise, -3.0, 3.0, (NC, NC), jnp.float32)
    diagonal_values = jax.random.uniform(key_diag, (NC,), jnp.float32, 2.0, 4.0)
    return assemble(noise, diagonal_values, NC)


def with_ends(array, own_key, least, top_value):
    extent = array.shape
    place = [jax.random.randint(jax.random.fold_in(own_key, axis), (), 0, extent[axis]) for axis in range(len(extent))]
    array = array.at[tuple(place)].set(least)
    longest = extent.index(max(extent))
    place[longest] = (place[longest] + 1) % extent[longest]
    return array.at[tuple(place)].set(top_value)


def block_levels(own_key, extent, pieces, low, high):
    level, own = 1.0, jax.random.fold_in(own_key, 6)
    for dim, shards_of in pieces:
        heights = jnp.exp(jax.random.uniform(jax.random.fold_in(own, dim), (shards_of,), jnp.float32, low / len(pieces), high / len(pieces)))
        level = level * jnp.repeat(heights, extent[dim] // shards_of).reshape([-1 if axis == dim else 1 for axis in range(len(extent))])
    return level


def normal_values(own_key, shape, scale, reach, cuts=(), held_as=jnp.bfloat16):
    factor_of = block_levels(own_key, shape, cuts, -0.22, 0.18) if cuts else 1.0
    entries = jax.random.normal(own_key, shape, jnp.float32) * scale * factor_of
    return jnp.minimum(jnp.maximum(entries, -reach), reach).astype(held_as)


def setup_inputs(seed: int = 0) -> dict:
    key_of = jax.random.split(jax.random.key(seed), 8)
    flex = draw_flex(jax.random.fold_in(key_of[7], 71), 0)
    precond = draw_precond(jax.random.fold_in(key_of[7], 71), 0)
    corner_map = normal_values(key_of[2], (SPANS, DECKS, NC, IFACE), IFACE ** -0.5, 0.1875, ((0, 32), (1, 8)), jnp.float32)
    coarse_inverse = draw_coarse_inverse(jax.random.fold_in(key_of[7], 71), 0)
    gap_deck = normal_values(key_of[4], (SPANS, DECKS, CASES, FACE), 1.0, 6.0, ((0, 32), (1, 8)), jnp.float32)
    gap_joint = normal_values(key_of[5], (SPANS, DECKS, CASES, FACE), 1.0, 6.0, ((0, 32), (1, 8)), jnp.float32)
    active = with_ends((jax.random.randint(key_of[6], (SPANS, DECKS, GB), 0, 2) < 1).astype(jnp.int32), jax.random.fold_in(key_of[6], 1), 0, 1)
    return dict(flex=flex, precond=precond, corner_map=corner_map, coarse_inverse=coarse_inverse, gap_deck=gap_deck, gap_joint=gap_joint, active=active)


HIGH = lax.Precision.HIGHEST

def from_lower(values, along):
    edge = jnp.zeros_like(lax.slice_in_dim(values, 0, 1, axis=along))
    return jnp.concatenate([edge, lax.slice_in_dim(values, 0, values.shape[along] - 1, axis=along)], along)

def from_upper(values, along):
    edge = jnp.zeros_like(lax.slice_in_dim(values, 0, 1, axis=along))
    return jnp.concatenate([lax.slice_in_dim(values, 1, values.shape[along], axis=along), edge], along)

def spread(deck_part, joint_part):
    return jnp.concatenate([deck_part, -from_lower(deck_part, 1), joint_part, -from_lower(joint_part, 0)], axis=3)

def collect(field, deck_live, joint_live):
    quarter = field.shape[3] // 4
    right = field[..., :quarter]
    left = field[..., quarter:2 * quarter]
    ahead = field[..., 2 * quarter:3 * quarter]
    behind = field[..., 3 * quarter:]
    return (deck_live * (right - from_upper(left, 1)), joint_live * (ahead - from_upper(behind, 0)))

def inner_sum(first_deck, first_joint, second_deck, second_joint):
    return lax.optimization_barrier(jnp.sum(first_deck * second_deck, axis=(0, 1, 3))) + lax.optimization_barrier(jnp.sum(first_joint * second_joint, axis=(0, 1, 3)))

def reference(flex, precond, corner_map, coarse_inverse, gap_deck, gap_joint, active):
    block_width = FACE // GB
    joint_live = jnp.repeat(active.astype(jnp.float32), block_width, axis=2)
    span_alive = (jnp.arange(SPANS) < SPANS - 1).astype(jnp.float32)
    joint_live = (joint_live * span_alive[:, None, None])[:, :, None, :]
    deck_alive = (jnp.arange(DECKS) < DECKS - 1).astype(jnp.float32)
    deck_live = deck_alive[None, :, None, None]
    coarse_scale = 1.0 / math.sqrt(SPANS * DECKS)

    def operator(dir_deck, dir_joint):
        jumps = spread(dir_deck, dir_joint)
        local_part = jnp.einsum('sdci,sdij->sdcj', jumps, flex, precision=HIGH)
        corner_total = jnp.einsum('sdci,sdki->ck', jumps, corner_map, precision=HIGH)
        corner_load = coarse_scale * jnp.dot(corner_total, coarse_inverse, precision=HIGH)
        field = local_part + jnp.einsum('ck,sdki->sdci', corner_load, corner_map, precision=HIGH)
        return collect(field, deck_live, joint_live)

    def precondition(res_deck, res_joint):
        jumps = spread(res_deck, res_joint)
        smoothed = jnp.einsum('sdci,sdij->sdcj', jumps, precond, precision=HIGH)
        out_deck, out_joint = collect(smoothed, deck_live, joint_live)
        return (0.5 * out_deck, 0.5 * out_joint)
    res_deck = deck_live * gap_deck
    res_joint = joint_live * gap_joint
    sol_deck = jnp.zeros_like(res_deck)
    sol_joint = jnp.zeros_like(res_joint)
    pre_deck, pre_joint = precondition(res_deck, res_joint)
    dir_deck, dir_joint = (pre_deck, pre_joint)
    resid_dot = inner_sum(res_deck, res_joint, pre_deck, pre_joint)
    for iteration in range(ITERS):
        image_deck, image_joint = operator(dir_deck, dir_joint)
        curvature = inner_sum(dir_deck, dir_joint, image_deck, image_joint)
        step_length = (resid_dot / curvature)[None, None, :, None]
        sol_deck = sol_deck + step_length * dir_deck
        sol_joint = sol_joint + step_length * dir_joint
        res_deck = res_deck - step_length * image_deck
        res_joint = res_joint - step_length * image_joint
        if iteration + 1 < ITERS:
            pre_deck, pre_joint = precondition(res_deck, res_joint)
            new_dot = inner_sum(res_deck, res_joint, pre_deck, pre_joint)
            ratio = (new_dot / resid_dot)[None, None, :, None]
            dir_deck = pre_deck + ratio * dir_deck
            dir_joint = pre_joint + ratio * dir_joint
            resid_dot = new_dot
    return (sol_deck, sol_joint, res_deck, res_joint)
```

```python
import math

import jax
import jax.numpy as jnp
from jax import lax
from jax.sharding import PartitionSpec as P

HIGH = lax.Precision.HIGH
AXES = ("span", "deck")
DEVICES = 256
CORE, X, Y, Z = (1, 2), (2, 4), (8, 4), (32, 8)


def shifted(block, place, k):
    stride, size = place
    route = []
    for i in range(DEVICES):
        digit = (i // stride) % size
        route.append((i, i + ((digit + k) % size - digit) * stride))
    return lax.ppermute(block, AXES, route)


def cyclic(block, axis, k):
    n = lax.axis_size(axis)
    return lax.ppermute(block, axis, [(i, (i + k) % n) for i in range(n)])


def matmul(left, right):
    return jnp.dot(left, right, precision=HIGH, preferred_element_type=jnp.float32)


def matmul_trans(left, right):
    return lax.dot_general(
        left, right, (((1,), (1,)), ((), ())), precision=HIGH, preferred_element_type=jnp.float32
    )


def row_dot(left, right):
    return jnp.sum(left * right, axis=1, keepdims=True)


def rows(block, index, count):
    return lax.dynamic_slice_in_dim(block, index * count, count, axis=0)


def reduce_rows(block, core, x):
    half = block.shape[0] // 2
    block = rows(block, core, half) + shifted(rows(block, 1 - core, half), CORE, 1)
    piece = half // 4
    sent = [shifted(rows(block, (x + k) % 4, piece), X, k) for k in (1, 2, 3)]
    part = rows(block, x, piece) + sent[0] + sent[1] + sent[2]
    got = [shifted(part, Y, k) for k in (1, 2, 3)]
    part = part + got[0] + got[1] + got[2]
    low, high = shifted(part, Z, 1), shifted(part, Z, -1)
    two = part + low
    three = two + high
    return three + shifted(three, Z, -3) + shifted(two, Z, 2)


def gather_rows(part, core, x):
    got = [shifted(part, X, k) for k in (1, 2, 3)]
    turned = jnp.concatenate([part, got[2], got[1], got[0]], axis=0)
    turned = jnp.concatenate([turned, turned], axis=0)
    half = rows(turned, (4 - x) % 4, part.shape[0])
    half = lax.dynamic_slice_in_dim(turned, ((4 - x) % 4) * part.shape[0], 4 * part.shape[0], axis=0)
    other = shifted(half, CORE, 1)
    return jnp.where(
        core == 0,
        jnp.concatenate([half, other], axis=0),
        jnp.concatenate([other, half], axis=0),
    )


def local(flex, precond, corner_map, coarse_inverse, gap_deck, gap_joint, active):
    flex_local = flex[0, 0]
    pre_local = precond[0, 0]
    corners = corner_map[0, 0]
    blocks = active[0, 0]
    face = gap_deck.shape[3]
    span, deck = lax.axis_index("span"), lax.axis_index("deck")
    core, x = deck % 2, deck // 2
    scale = 1.0 / math.sqrt(lax.axis_size("span") * lax.axis_size("deck"))

    span_alive = (span < lax.axis_size("span") - 1).astype(jnp.float32)
    joint_live = (jnp.repeat(blocks.astype(jnp.float32), face // blocks.shape[0]) * span_alive)[None, :]
    deck_live = (deck < lax.axis_size("deck") - 1).astype(jnp.float32)
    deck_live_behind = (deck > 0).astype(jnp.float32)

    def quarters(field):
        return [field[:, i * face : (i + 1) * face] for i in range(4)]

    def jump_of_reaction(field):
        right, left, ahead, behind = quarters(field)
        from_span = cyclic(ahead, "span", 1), cyclic(behind, "span", -1)
        from_deck = cyclic(right, "deck", 1), cyclic(left, "deck", -1)
        return jnp.concatenate(
            [
                deck_live * (right - from_deck[1]),
                deck_live_behind * (left - from_deck[0]),
                joint_live * (ahead - from_span[1]),
                joint_live_behind * (behind - from_span[0]),
            ],
            axis=1,
        )

    def reaction(field):
        right, left, ahead, behind = quarters(field)
        return (
            deck_live * (right - cyclic(left, "deck", -1)),
            joint_live * (ahead - cyclic(behind, "span", -1)),
        )

    def faces(jump):
        first, _, third, _ = quarters(jump)
        return first, third

    res_deck = deck_live * gap_deck[0, 0]
    res_joint = joint_live * gap_joint[0, 0]
    sent = jnp.concatenate([res_joint, jnp.broadcast_to(joint_live, (8, face))], axis=0)
    got = cyclic(sent, "span", 1)
    joint_live_behind = got[res_joint.shape[0]][None, :]
    res_jump = jnp.concatenate(
        [res_deck, -cyclic(res_deck, "deck", 1), res_joint, -got[: res_joint.shape[0]]], axis=1
    )

    corner_jump = jump_of_reaction(corners)
    corner_deck, corner_joint = faces(corner_jump)

    def corner_sum(part_deck, part_joint):
        return matmul_trans(part_deck, corner_deck) + matmul_trans(part_joint, corner_joint)

    def table(total, *columns):
        pad = jnp.zeros((total.shape[0], 128 - len(columns)), jnp.float32)
        return jnp.concatenate([total, *columns, pad], axis=1)

    nc = coarse_inverse.shape[0]

    z_jump = jump_of_reaction(matmul(res_jump, 0.5 * pre_local))
    z_deck, z_joint = faces(z_jump)
    z_field = matmul(z_jump, flex_local)
    rz = row_dot(res_deck, z_deck) + row_dot(res_joint, z_joint)
    part = reduce_rows(
        table(corner_sum(z_deck, z_joint), rz, row_dot(z_jump, z_field)), core, x
    )
    total, rz, curv = part[:, :nc], part[:, nc : nc + 1], part[:, nc + 1 : nc + 2]
    load = scale * matmul(total, coarse_inverse)
    curv = curv + row_dot(load, total)
    whole = gather_rows(table(load, rz / curv), core, x)
    load, step = whole[:, :nc], whole[:, nc : nc + 1]

    image_jump = jump_of_reaction(z_field) + matmul(load, corner_jump)
    image_deck, image_joint = faces(image_jump)
    res_jump = res_jump - step * image_jump
    res_deck, res_joint = faces(res_jump)

    y_jump = jump_of_reaction(matmul(res_jump, 0.5 * pre_local))
    y_deck, y_joint = faces(y_jump)
    y_field = matmul(y_jump, flex_local)
    part = reduce_rows(
        table(
            corner_sum(y_deck, y_joint),
            row_dot(res_deck, y_deck) + row_dot(res_joint, y_joint),
            row_dot(y_jump, y_field),
            row_dot(y_deck, image_deck) + row_dot(y_joint, image_joint),
        ),
        core,
        x,
    )
    total = part[:, :nc]
    new, own, cross = (part[:, nc + i : nc + i + 1] for i in range(3))
    load = scale * matmul(total, coarse_inverse)
    own = own + row_dot(load, total)
    ratio = new / rz
    second = new / (own + ratio * (2.0 * cross + ratio * curv))
    whole = gather_rows(table(second * load, second, second * ratio), core, x)
    load = whole[:, :nc]
    second, mixed = whole[:, nc : nc + 1], whole[:, nc + 1 : nc + 2]

    field_deck, field_joint = reaction(y_field)
    first = step + mixed
    sol_deck = first * z_deck + second * y_deck
    sol_joint = first * z_joint + second * y_joint
    out_deck = res_deck - second * field_deck - mixed * image_deck - matmul(load, corner_deck)
    out_joint = res_joint - second * field_joint - mixed * image_joint - matmul(load, corner_joint)
    return (
        sol_deck[None, None],
        sol_joint[None, None],
        out_deck[None, None],
        out_joint[None, None],
    )


def solution(mesh):
    block = P("span", "deck", None, None)
    in_specs = (block, block, block, P(), block, block, P("span", "deck", None))
    return jax.shard_map(
        local, mesh=mesh, in_specs=in_specs, out_specs=(block,) * 4, check_vma=False
    )
```

```python
import functools
import math

import jax
import jax.numpy as jnp
from jax import lax
from jax.experimental import pallas as pl
from jax.experimental.pallas import tpu as pltpu
from jax.sharding import PartitionSpec as P

AXES = ("span", "deck")
SPANS, DECKS, DEVICES = 32, 8, 256
CORE, X, Y, Z = (1, 2), (2, 4), (8, 4), (32, 8)
CASES, FACE, IFACE, NC, GB = 256, 256, 1024, 256, 4
WIDE = NC + 128
PIECE = 32
SCALE = 1.0 / math.sqrt(SPANS * DECKS)
F32, BF16 = jnp.float32, jnp.bfloat16
VMEM = pl.BlockSpec(memory_space=pltpu.VMEM)
SMEM = pl.BlockSpec(memory_space=pltpu.SMEM)


def shifted(block, place, k):
    stride, size = place
    route = []
    for i in range(DEVICES):
        digit = (i // stride) % size
        route.append((i, i + ((digit + k) % size - digit) * stride))
    return lax.ppermute(block, AXES, route)


def cyclic(block, axis, k):
    n = lax.axis_size(axis)
    return lax.ppermute(block, axis, [(i, (i + k) % n) for i in range(n)])


def parts(value):
    high = value.astype(BF16)
    return high, (value - high.astype(F32)).astype(BF16)


def product(left, right, dims=(((1,), (0,)), ((), ()))):
    dot = functools.partial(lax.dot_general, dimension_numbers=dims, preferred_element_type=F32)
    return dot(left[0], right[0]) + (dot(left[0], right[1]) + dot(left[1], right[0]))


TRANS = (((1,), (1,)), ((), ()))


def quarter(ref, i):
    return ref[:, i * FACE : (i + 1) * FACE]


def column(lane, *values):
    out = jnp.zeros((values[0].shape[0], 128), F32)
    for i, value in enumerate(values):
        out = jnp.where(lane == i, value, out)
    return out


def row_sum(value):
    return jnp.sum(value, axis=1, keepdims=True)


def cost(rows):
    return pl.CostEstimate(flops=6 * rows * IFACE * IFACE, bytes_accessed=8 << 20, transcendentals=0)


def call(body, outs, n_in, name, smem=(), scratch=(), estimate=None):
    return pl.pallas_call(
        body,
        out_shape=tuple(jax.ShapeDtypeStruct(s, F32) for s in outs),
        in_specs=[SMEM if i in smem else VMEM for i in range(n_in)],
        out_specs=tuple(VMEM for _ in outs),
        scratch_shapes=list(scratch),
        compiler_params=pltpu.CompilerParams(vmem_limit_bytes=24 << 20),
        cost_estimate=estimate,
        name=name,
    )


def times_matrix(u_high, u_low, matrix_ref, store):
    for i in range(4):
        store(i, product((u_high[...], u_low[...]), parts(quarter(matrix_ref, i))))


def keep(u_high, u_low, i, value):
    high, low = parts(value)
    u_high[:, i * FACE : (i + 1) * FACE] = high
    u_low[:, i * FACE : (i + 1) * FACE] = low


U_SCRATCH = (pltpu.VMEM((CASES, IFACE), BF16), pltpu.VMEM((CASES, IFACE), BF16))


def start_kernel(place, active, active_behind, deck, joint, deck_behind, joint_behind, matrix,
                 v0, v1, v2, v3, masks, u_high, u_low):
    span, across = place[0], place[1]
    block = lax.broadcasted_iota(jnp.int32, (1, FACE), 1) // (FACE // GB)

    def live(ref, on):
        row = jnp.zeros((1, FACE), F32)
        for b in range(GB):
            row = jnp.where(block == b, ref[b].astype(F32), row)
        return row * on.astype(F32)

    ones = jnp.ones((1, FACE), F32)
    lives = (
        ones * (across < DECKS - 1).astype(F32),
        ones * (across > 0).astype(F32),
        live(active, span < SPANS - 1),
        live(active_behind, span > 0),
    )
    masks[...] = jnp.concatenate(lives + (jnp.zeros((4, FACE), F32),), axis=0)
    keep(u_high, u_low, 0, lives[0] * deck[...])
    keep(u_high, u_low, 1, -(lives[1] * deck_behind[...]))
    keep(u_high, u_low, 2, lives[2] * joint[...])
    keep(u_high, u_low, 3, -(lives[3] * joint_behind[...]))

    def store(i, value):
        (v0, v1, v2, v3)[i][...] = 0.5 * value

    times_matrix(u_high, u_low, matrix, store)


def jump(masks, own, got, i):
    return masks[i : i + 1, :] * (own[i][: CASES, :] - got[i][: CASES, :])


def flex_kernel(n_faces, place, masks, f0, f1, f2, f3, g0, g1, g2, g3, matrix, corners, *refs):
    pairs, refs = refs[: 2 * n_faces], refs[2 * n_faces :]
    outs, (first, third, sent, held, u_high, u_low, u_full, table) = refs[:4], refs[4:]
    core, x = lax.rem(place[1], 2), place[1] // 2
    own, got = (f0, f1, f2, f3), (g0, g1, g2, g3)
    for i in range(4):
        value = jump(masks, own, got, i)
        keep(u_high, u_low, i, value)
        u_full[:, i * FACE : (i + 1) * FACE] = value
    first[...] = quarter(u_full, 0)
    third[...] = quarter(u_full, 2)
    total = jnp.zeros((CASES, 1), F32)
    for i in range(4):
        value = product((u_high[...], u_low[...]), parts(quarter(matrix, i)))
        total = total + row_sum(quarter(u_full, i) * value)
        if outs[i].shape[0] == CASES:
            outs[i][...] = value
        else:
            outs[i][: CASES, :] = value
            outs[i][CASES:, :] = quarter(corners, i)
    sums = [
        row_sum(masks[0:1, :] * pairs[2 * k][...] * first[...] + masks[2:3, :] * pairs[2 * k + 1][...] * third[...])
        for k in range(n_faces)
    ]
    table[:, :NC] = product((u_high[...], u_low[...]), parts(corners[...]), TRANS)
    lane = lax.broadcasted_iota(jnp.int32, (CASES, 128), 1)
    table[:, NC:] = column(lane, total, *sums)
    for k in range(4):
        turn = lax.rem(x + k, 4)
        at = pl.ds(k * PIECE, PIECE)
        held[at, :] = table[pl.ds(pl.multiple_of((core * 4 + turn) * PIECE, PIECE), PIECE), :]
        sent[at, :] = table[pl.ds(pl.multiple_of(((1 - core) * 4 + turn) * PIECE, PIECE), PIECE), :]


def first_coarse_kernel(three, a, b, coarse, out, scalars):
    part = three[...] + a[...] + b[...]
    total = part[:, :NC]
    load = SCALE * product(parts(total), parts(coarse[...]))
    curv = part[:, NC : NC + 1] + row_sum(load * total)
    rz = part[:, NC + 1 : NC + 2]
    lane = lax.broadcasted_iota(jnp.int32, (PIECE, 128), 1)
    out[:, :NC] = load
    out[:, NC:] = column(lane, rz / curv)
    scalars[...] = column(lane, rz, curv)


def second_coarse_kernel(three, a, b, coarse, scalars, out):
    part = three[...] + a[...] + b[...]
    total = part[:, :NC]
    load = SCALE * product(parts(total), parts(coarse[...]))
    own = part[:, NC : NC + 1] + row_sum(load * total)
    new = part[:, NC + 1 : NC + 2]
    cross = part[:, NC + 2 : NC + 3]
    rz, curv = scalars[:, 0:1], scalars[:, 1:2]
    ratio = new / rz
    second = new / (own + ratio * (2.0 * cross + ratio * curv))
    lane = lax.broadcasted_iota(jnp.int32, (PIECE, 128), 1)
    out[:, :NC] = second * load
    out[:, NC:] = column(lane, second, second * ratio)


def place_rows(place, pieces, whole):
    core, x = lax.rem(place[1], 2), place[1] // 2
    for k, piece in enumerate(pieces):
        turn = lax.rem(x + 4 - k, 4)
        whole[pl.ds(pl.multiple_of((core * 4 + turn) * PIECE, PIECE), PIECE), :] = piece[:PIECE, :]
        whole[pl.ds(pl.multiple_of(((1 - core) * 4 + turn) * PIECE, PIECE), PIECE), :] = piece[PIECE:, :]


def precond_kernel(place, masks, p0, p1, p2, p3, f0, f1, f2, f3, g0, g1, g2, g3,
                   deck, joint, deck_behind, joint_behind, matrix,
                   v0, v1, v2, v3, image_deck, image_joint, res_deck, res_joint,
                   corner_deck, corner_joint, steps, u_high, u_low, whole):
    place_rows(place, (p0, p1, p2, p3), whole)
    load = parts(whole[:, :NC])
    step = whole[:, NC : NC + 1]
    steps[...] = whole[:, NC:]
    own, got = (f0, f1, f2, f3), (g0, g1, g2, g3)
    gaps = (deck, deck_behind, joint, joint_behind)
    for i in range(4):
        live = masks[i : i + 1, :]
        corner = live * (own[i][CASES:, :] - got[i][CASES:, :])
        image = jump(masks, own, got, i) + product(load, parts(corner))
        gap = live * gaps[i][...]
        res = (gap if i % 2 == 0 else -gap) - step * image
        if i == 0:
            corner_deck[...], image_deck[...], res_deck[...] = corner, image, res
        if i == 2:
            corner_joint[...], image_joint[...], res_joint[...] = corner, image, res
        keep(u_high, u_low, i, res)

    def store(i, value):
        (v0, v1, v2, v3)[i][...] = 0.5 * value

    times_matrix(u_high, u_low, matrix, store)


def final_kernel(place, masks, p0, p1, p2, p3, steps, z_deck, z_joint, y_deck, y_joint,
                 image_deck, image_joint, res_deck, res_joint, corner_deck, corner_joint,
                 f0, f2, g0, g2, sol_deck, sol_joint, out_deck, out_joint, whole):
    place_rows(place, (p0, p1, p2, p3), whole)
    load = parts(whole[:, :NC])
    second, mixed = whole[:, NC : NC + 1], whole[:, NC + 1 : NC + 2]
    first = steps[:, 0:1] + mixed
    sol_deck[...] = first * z_deck[...] + second * y_deck[...]
    sol_joint[...] = first * z_joint[...] + second * y_joint[...]
    for i, res, field, ahead, image, corner, out in (
        (0, res_deck, f0, g0, image_deck, corner_deck, out_deck),
        (2, res_joint, f2, g2, image_joint, corner_joint, out_joint),
    ):
        reaction = masks[i : i + 1, :] * (field[...] - ahead[...])
        out[...] = (
            res[...] - second * reaction - mixed * image[...] - product(load, parts(corner[...]))
        )


def exchange(field):
    right, left, ahead, behind = field
    ahead_got, behind_got = cyclic(ahead, "span", 1), cyclic(behind, "span", -1)
    right_got, left_got = cyclic(right, "deck", 1), cyclic(left, "deck", -1)
    return left_got, right_got, behind_got, ahead_got


def reduce_rows(sent, held):
    block = held + shifted(sent, CORE, 1)
    piece = [block[k * PIECE : (k + 1) * PIECE] for k in range(4)]
    got = [shifted(piece[k], X, k) for k in (1, 2, 3)]
    part = piece[0] + got[0] + got[1] + got[2]
    got = [shifted(part, Y, k) for k in (1, 2, 3)]
    part = part + got[0] + got[1] + got[2]
    low, high = shifted(part, Z, 1), shifted(part, Z, -1)
    two = part + low
    three = two + high
    return three, shifted(three, Z, -3), shifted(two, Z, 2)


def gather_rows(part):
    pair = jnp.concatenate([part, shifted(part, CORE, 1)], axis=0)
    return [pair] + [shifted(pair, X, k) for k in (1, 2, 3)]


def after(values, *others):
    return lax.optimization_barrier((values, others))[0]


def local(flex, precond, corner_map, coarse_inverse, gap_deck, gap_joint, active):
    flex, precond, corners = flex[0, 0], precond[0, 0], corner_map[0, 0]
    deck, joint, active = gap_deck[0, 0], gap_joint[0, 0], active[0, 0]
    place = jnp.stack([lax.axis_index("span"), lax.axis_index("deck")]).astype(jnp.int32)

    face, field, stacked = (CASES, FACE), [(CASES, FACE)] * 4, [(2 * CASES, FACE)] * 4
    held, piece = (4 * PIECE, WIDE), (PIECE, WIDE)
    full = pltpu.VMEM((CASES, IFACE), F32)
    whole = pltpu.VMEM((CASES, WIDE), F32)

    joint_behind = cyclic(joint, "span", 1)
    deck_behind = cyclic(deck, "deck", 1)
    active_behind = cyclic(active, "span", 1)
    gaps = (deck, joint, deck_behind, joint_behind)
    *v, masks = call(
        start_kernel, field + [(8, FACE)], 8, "start", smem=(0, 1, 2), scratch=U_SCRATCH, estimate=cost(CASES)
    )(place, active, active_behind, *gaps, precond)
    *w, z_deck, z_joint, sent, kept = call(
        functools.partial(flex_kernel, 1), stacked + [face, face, held, held], 14, "flex_first",
        smem=(0,), scratch=U_SCRATCH + (full, whole), estimate=cost(CASES),
    )(place, masks, *v, *exchange(v), flex, corners, deck, joint)
    got = exchange(w)
    sums = reduce_rows(sent, kept)
    part, scalars = call(first_coarse_kernel, [piece, (PIECE, 128)], 4, "coarse_first")(
        *sums, coarse_inverse
    )
    part = after(part, got)
    *v, image_deck, image_joint, res_deck, res_joint, corner_deck, corner_joint, steps = call(
        precond_kernel, field + [face] * 6 + [(CASES, 128)], 19, "precond",
        smem=(0,), scratch=U_SCRATCH + (whole,), estimate=cost(CASES),
    )(place, masks, *gather_rows(part), *w, *got, *gaps, precond)
    *w, y_deck, y_joint, sent, kept = call(
        functools.partial(flex_kernel, 2), field + [face, face, held, held], 16, "flex_second",
        smem=(0,), scratch=U_SCRATCH + (full, whole), estimate=cost(CASES),
    )(place, masks, *v, *exchange(v), flex, corners, res_deck, res_joint, image_deck, image_joint)
    got = cyclic(w[1], "deck", -1), cyclic(w[3], "span", -1)
    sums = reduce_rows(sent, kept)
    (part,) = call(second_coarse_kernel, [piece], 5, "coarse_second")(*sums, coarse_inverse, scalars)
    part = after(part, got)
    outs = call(
        final_kernel, [face] * 4, 21, "final", smem=(0,), scratch=(whole,)
    )(
        place, masks, *gather_rows(part), steps, z_deck, z_joint, y_deck, y_joint,
        image_deck, image_joint, res_deck, res_joint, corner_deck, corner_joint, w[0], w[2], *got,
    )
    return tuple(out[None, None] for out in outs)


def solution(mesh):
    block = P("span", "deck", None, None)
    in_specs = (block, block, block, P(), block, block, P("span", "deck", None))
    return jax.shard_map(
        local, mesh=mesh, in_specs=in_specs, out_specs=(block,) * 4, check_vma=False
    )
```

```python
import functools
import math

import jax
import jax.numpy as jnp
from jax import lax
from jax.experimental import pallas as pl
from jax.experimental.pallas import tpu as pltpu
from jax.sharding import Mesh
from jax.sharding import PartitionSpec as P

SPAN, DECK = ("z", "y"), ("x", "core")
SPANS, DECKS, Y, X, Z = 32, 8, 4, 4, 8
CASES, FACE, IFACE, NC, GB = 256, 256, 1024, 256, 4
WIDE = NC + 128
HALF = CASES // 2
PIECE = HALF // (Y * X)
SCALE = 1.0 / math.sqrt(SPANS * DECKS)
F32, BF16 = jnp.float32, jnp.bfloat16
VMEM = pl.BlockSpec(memory_space=pltpu.VMEM)
SMEM = pl.BlockSpec(memory_space=pltpu.SMEM)


def cyclic(block, axes, k):
    n = SPANS if axes == SPAN else DECKS
    return lax.ppermute(block, axes, [(i, (i + k) % n) for i in range(n)])


def swapped(block):
    return lax.ppermute(block, "core", [(0, 1), (1, 0)])


def parts(value):
    high = value.astype(BF16)
    return high, (value - high.astype(F32)).astype(BF16)


def product(left, right, dims=(((1,), (0,)), ((), ()))):
    dot = functools.partial(lax.dot_general, dimension_numbers=dims, preferred_element_type=F32)
    return dot(left[0], right[0]) + (dot(left[0], right[1]) + dot(left[1], right[0]))


TRANS = (((1,), (1,)), ((), ()))


def quarter(ref, i):
    return ref[:, i * FACE : (i + 1) * FACE]


def column(lane, *values):
    out = jnp.zeros((values[0].shape[0], 128), F32)
    for i, value in enumerate(values):
        out = jnp.where(lane == i, value, out)
    return out


def row_sum(value):
    return jnp.sum(value, axis=1, keepdims=True)


def cost(rows):
    return pl.CostEstimate(flops=6 * rows * IFACE * IFACE, bytes_accessed=8 << 20, transcendentals=0)


def call(body, outs, n_in, name, smem=(), scratch=(), estimate=None):
    return pl.pallas_call(
        body,
        out_shape=tuple(jax.ShapeDtypeStruct(s, F32) for s in outs),
        in_specs=[SMEM if i in smem else VMEM for i in range(n_in)],
        out_specs=tuple(VMEM for _ in outs),
        scratch_shapes=list(scratch),
        compiler_params=pltpu.CompilerParams(vmem_limit_bytes=24 << 20),
        cost_estimate=estimate,
        name=name,
    )


def times_matrix(u_high, u_low, matrix_ref, store):
    for i in range(4):
        store(i, product((u_high[...], u_low[...]), parts(quarter(matrix_ref, i))))


def keep(u_high, u_low, i, value):
    high, low = parts(value)
    u_high[:, i * FACE : (i + 1) * FACE] = high
    u_low[:, i * FACE : (i + 1) * FACE] = low


U_SCRATCH = (pltpu.VMEM((CASES, IFACE), BF16), pltpu.VMEM((CASES, IFACE), BF16))


def live_row(ref, on):
    block = lax.broadcasted_iota(jnp.int32, (1, FACE), 1) // (FACE // GB)
    row = jnp.zeros((1, FACE), F32)
    for b in range(GB):
        row = jnp.where(block == b, ref[b].astype(F32), row)
    return row * on.astype(F32)


def faces_times(first, third, matrix, rows, i):
    at = slice(i * FACE, (i + 1) * FACE)
    return product(first, parts(matrix[rows : rows + FACE, at])) + product(
        third, parts(matrix[rows + 2 * FACE : rows + 3 * FACE, at])
    )


def own_kernel(place, active, deck, joint, matrix, part):
    span, across = place[0], place[1]
    first = parts((across < DECKS - 1).astype(F32) * deck[...])
    third = parts(live_row(active, span < SPANS - 1) * joint[...])
    for i in range(4):
        part[:, i * FACE : (i + 1) * FACE] = faces_times(first, third, matrix, 0, i)


def behind_kernel(place, active, active_behind, deck_behind, joint_behind, part, matrix,
                  v0, v1, v2, v3, masks):
    span, across = place[0], place[1]
    ones = jnp.ones((1, FACE), F32)
    lives = (
        ones * (across < DECKS - 1).astype(F32),
        ones * (across > 0).astype(F32),
        live_row(active, span < SPANS - 1),
        live_row(active_behind, span > 0),
    )
    masks[...] = jnp.concatenate(lives + (jnp.zeros((4, FACE), F32),), axis=0)
    second, fourth = parts(lives[1] * deck_behind[...]), parts(lives[3] * joint_behind[...])
    for i, out in enumerate((v0, v1, v2, v3)):
        out[...] = 0.5 * (quarter(part, i) - faces_times(second, fourth, matrix, FACE, i))


def jump(masks, own, got, i):
    return masks[i : i + 1, :] * (own[i][: CASES, :] - got[i][: CASES, :])


def flex_kernel(n_faces, place, masks, f0, f1, f2, f3, g0, g1, g2, g3, matrix, corners, *refs):
    pairs, refs = refs[: 2 * n_faces], refs[2 * n_faces :]
    outs, (first, third, sent, held, u_high, u_low, u_full, table) = refs[:4], refs[4:]
    core = lax.rem(place[1], 2)
    own, got = (f0, f1, f2, f3), (g0, g1, g2, g3)
    for i in range(4):
        value = jump(masks, own, got, i)
        keep(u_high, u_low, i, value)
        u_full[:, i * FACE : (i + 1) * FACE] = value
    first[...] = quarter(u_full, 0)
    third[...] = quarter(u_full, 2)
    total = jnp.zeros((CASES, 1), F32)
    for i in range(4):
        value = product((u_high[...], u_low[...]), parts(quarter(matrix, i)))
        total = total + row_sum(quarter(u_full, i) * value)
        if outs[i].shape[0] == CASES:
            outs[i][...] = value
        else:
            outs[i][: CASES, :] = value
            outs[i][CASES:, :] = quarter(corners, i)
    sums = [
        row_sum(masks[0:1, :] * pairs[2 * k][...] * first[...] + masks[2:3, :] * pairs[2 * k + 1][...] * third[...])
        for k in range(n_faces)
    ]
    table[:, :NC] = product((u_high[...], u_low[...]), parts(corners[...]), TRANS)
    lane = lax.broadcasted_iota(jnp.int32, (CASES, 128), 1)
    table[:, NC:] = column(lane, total, *sums)
    held[...] = table[pl.ds(pl.multiple_of(core * HALF, HALF), HALF), :]
    sent[...] = table[pl.ds(pl.multiple_of((1 - core) * HALF, HALF), HALF), :]


def total_of(got):
    part = got[0]
    for k in range(1, Z):
        part = part + got[k]
    return part


def first_coarse_kernel(got, coarse, out, scalars):
    part = total_of(got)
    total = part[:, :NC]
    load = SCALE * product(parts(total), parts(coarse[...]))
    curv = part[:, NC : NC + 1] + row_sum(load * total)
    rz = part[:, NC + 1 : NC + 2]
    lane = lax.broadcasted_iota(jnp.int32, (PIECE, 128), 1)
    row = jnp.concatenate([load, column(lane, rz / curv)], axis=1)
    for k in range(Y * X):
        out[k] = row
    scalars[...] = column(lane, rz, curv)


def second_coarse_kernel(got, coarse, scalars, out):
    part = total_of(got)
    total = part[:, :NC]
    load = SCALE * product(parts(total), parts(coarse[...]))
    own = part[:, NC : NC + 1] + row_sum(load * total)
    new = part[:, NC + 1 : NC + 2]
    cross = part[:, NC + 2 : NC + 3]
    rz, curv = scalars[:, 0:1], scalars[:, 1:2]
    ratio = new / rz
    second = new / (own + ratio * (2.0 * cross + ratio * curv))
    lane = lax.broadcasted_iota(jnp.int32, (PIECE, 128), 1)
    row = jnp.concatenate([second * load, column(lane, second, second * ratio)], axis=1)
    for k in range(Y * X):
        out[k] = row


def place_rows(place, mine, other, whole):
    core = lax.rem(place[1], 2)
    whole[pl.ds(pl.multiple_of(core * HALF, HALF), HALF), :] = mine[...]
    whole[pl.ds(pl.multiple_of((1 - core) * HALF, HALF), HALF), :] = other[...]


def precond_kernel(place, masks, mine, other, f0, f1, f2, f3, g0, g1, g2, g3,
                   deck, joint, deck_behind, joint_behind, matrix,
                   v0, v1, v2, v3, image_deck, image_joint, res_deck, res_joint,
                   corner_deck, corner_joint, steps, u_high, u_low, whole):
    place_rows(place, mine, other, whole)
    load = parts(whole[:, :NC])
    step = whole[:, NC : NC + 1]
    steps[...] = whole[:, NC:]
    own, got = (f0, f1, f2, f3), (g0, g1, g2, g3)
    gaps = (deck, deck_behind, joint, joint_behind)
    for i in range(4):
        live = masks[i : i + 1, :]
        corner = live * (own[i][CASES:, :] - got[i][CASES:, :])
        image = jump(masks, own, got, i) + product(load, parts(corner))
        gap = live * gaps[i][...]
        res = (gap if i % 2 == 0 else -gap) - step * image
        if i == 0:
            corner_deck[...], image_deck[...], res_deck[...] = corner, image, res
        if i == 2:
            corner_joint[...], image_joint[...], res_joint[...] = corner, image, res
        keep(u_high, u_low, i, res)

    def store(i, value):
        (v0, v1, v2, v3)[i][...] = 0.5 * value

    times_matrix(u_high, u_low, matrix, store)


def final_kernel(place, masks, mine, other, steps, z_deck, z_joint, y_deck, y_joint,
                 image_deck, image_joint, res_deck, res_joint, corner_deck, corner_joint,
                 f0, f2, g0, g2, sol_deck, sol_joint, out_deck, out_joint, whole):
    place_rows(place, mine, other, whole)
    load = parts(whole[:, :NC])
    second, mixed = whole[:, NC : NC + 1], whole[:, NC + 1 : NC + 2]
    first = steps[:, 0:1] + mixed
    sol_deck[...] = first * z_deck[...] + second * y_deck[...]
    sol_joint[...] = first * z_joint[...] + second * y_joint[...]
    for i, res, field, ahead, image, corner, out in (
        (0, res_deck, f0, g0, image_deck, corner_deck, out_deck),
        (2, res_joint, f2, g2, image_joint, corner_joint, out_joint),
    ):
        reaction = masks[i : i + 1, :] * (field[...] - ahead[...])
        out[...] = (
            res[...] - second * reaction - mixed * image[...] - product(load, parts(corner[...]))
        )


def exchange(field):
    right, left, ahead, behind = field
    ahead_got, behind_got = cyclic(ahead, SPAN, 1), cyclic(behind, SPAN, -1)
    right_got, left_got = cyclic(right, DECK, 1), cyclic(left, DECK, -1)
    return left_got, right_got, behind_got, ahead_got


def reduce_rows(sent, held):
    block = held + swapped(sent)
    got = lax.all_to_all(block.reshape(Y * X, PIECE, WIDE), ("y", "x"), 0, 0)
    part = jnp.sum(got, axis=0)
    return lax.all_to_all(jnp.broadcast_to(part, (Z, PIECE, WIDE)), "z", 0, 0)


def gather_rows(copies):
    mine = lax.all_to_all(copies, ("y", "x"), 0, 0).reshape(HALF, WIDE)
    return mine, swapped(mine)


def after(values, *others):
    return lax.optimization_barrier((values, others))[0]


def local(flex, precond, corner_map, coarse_inverse, gap_deck, gap_joint, active):
    flex, precond, corners = flex[0, 0], precond[0, 0], corner_map[0, 0]
    deck, joint, active = gap_deck[0, 0], gap_joint[0, 0], active[0, 0]
    span = lax.axis_index("z") * Y + lax.axis_index("y")
    across = lax.axis_index("x") * 2 + lax.axis_index("core")
    place = jnp.stack([span, across]).astype(jnp.int32)

    face, field, stacked = (CASES, FACE), [(CASES, FACE)] * 4, [(2 * CASES, FACE)] * 4
    half, copies = (HALF, WIDE), (Y * X, PIECE, WIDE)
    full = pltpu.VMEM((CASES, IFACE), F32)
    whole = pltpu.VMEM((CASES, WIDE), F32)

    joint_behind = cyclic(joint, SPAN, 1)
    deck_behind = cyclic(deck, DECK, 1)
    active_behind = cyclic(active, SPAN, 1)
    gaps = (deck, joint, deck_behind, joint_behind)
    (part,) = call(
        own_kernel, [(CASES, IFACE)], 5, "own", smem=(0, 1), estimate=cost(CASES // 2)
    )(place, active, deck, joint, precond)
    *v, masks = call(
        behind_kernel, field + [(8, FACE)], 7, "behind", smem=(0, 1, 2), estimate=cost(CASES // 2)
    )(place, active, active_behind, deck_behind, joint_behind, part, precond)
    *w, z_deck, z_joint, sent, held = call(
        functools.partial(flex_kernel, 1), stacked + [face, face, half, half], 14, "flex_first",
        smem=(0,), scratch=U_SCRATCH + (full, whole), estimate=cost(CASES),
    )(place, masks, *v, *exchange(v), flex, corners, deck, joint)
    got = exchange(w)
    sums = reduce_rows(sent, held)
    loads, scalars = call(first_coarse_kernel, [copies, (PIECE, 128)], 2, "coarse_first")(
        sums, coarse_inverse
    )
    loads = after(loads, got)
    *v, image_deck, image_joint, res_deck, res_joint, corner_deck, corner_joint, steps = call(
        precond_kernel, field + [face] * 6 + [(CASES, 128)], 17, "precond",
        smem=(0,), scratch=U_SCRATCH + (whole,), estimate=cost(CASES),
    )(place, masks, *gather_rows(loads), *w, *got, *gaps, precond)
    *w, y_deck, y_joint, sent, held = call(
        functools.partial(flex_kernel, 2), field + [face, face, half, half], 16, "flex_second",
        smem=(0,), scratch=U_SCRATCH + (full, whole), estimate=cost(CASES),
    )(place, masks, *v, *exchange(v), flex, corners, res_deck, res_joint, image_deck, image_joint)
    got = cyclic(w[1], DECK, -1), cyclic(w[3], SPAN, -1)
    sums = reduce_rows(sent, held)
    (loads,) = call(second_coarse_kernel, [copies], 3, "coarse_second")(sums, coarse_inverse, scalars)
    loads = after(loads, got)
    outs = call(
        final_kernel, [face] * 4, 19, "final", smem=(0,), scratch=(whole,)
    )(
        place, masks, *gather_rows(loads), steps, z_deck, z_joint, y_deck, y_joint,
        image_deck, image_joint, res_deck, res_joint, corner_deck, corner_joint, w[0], w[2], *got,
    )
    return tuple(out[None, None] for out in outs)


def solution(mesh):
    mesh = Mesh(mesh.devices.reshape(Z, Y, X, 2), SPAN + DECK)
    block = P(SPAN, DECK, None, None)
    in_specs = (block, block, block, P(), block, block, P(SPAN, DECK, None))
    return jax.shard_map(
        local, mesh=mesh, in_specs=in_specs, out_specs=(block,) * 4, check_vma=False
    )
```

```python
import functools
import math

import jax
import jax.numpy as jnp
from jax import lax
from jax.experimental import pallas as pl
from jax.experimental.pallas import tpu as pltpu
from jax.sharding import Mesh
from jax.sharding import PartitionSpec as P

SPAN, DECK = ("z", "y"), ("x", "core")
SPANS, DECKS, Y, X, Z = 32, 8, 4, 4, 8
CASES, FACE, IFACE, NC, GB = 256, 256, 1024, 256, 4
WIDE = NC + 128
HALF = CASES // 2
PIECE = HALF // (Y * X)
SCALE = 1.0 / math.sqrt(SPANS * DECKS)
F32, BF16 = jnp.float32, jnp.bfloat16
VMEM = pl.BlockSpec(memory_space=pltpu.VMEM)
SMEM = pl.BlockSpec(memory_space=pltpu.SMEM)


def cyclic(block, axes, k):
    n = SPANS if axes == SPAN else DECKS
    return lax.ppermute(block, axes, [(i, (i + k) % n) for i in range(n)])


def swapped(block):
    return lax.ppermute(block, "core", [(0, 1), (1, 0)])


def parts(value):
    high = value.astype(BF16)
    return high, (value - high.astype(F32)).astype(BF16)


def product(left, right, dims=(((1,), (0,)), ((), ()))):
    dot = functools.partial(lax.dot_general, dimension_numbers=dims, preferred_element_type=F32)
    return dot(left[0], right[0]) + (dot(left[0], right[1]) + dot(left[1], right[0]))


TRANS = (((1,), (1,)), ((), ()))


def quarter(ref, i):
    return ref[:, i * FACE : (i + 1) * FACE]


def column(lane, *values):
    out = jnp.zeros((values[0].shape[0], 128), F32)
    for i, value in enumerate(values):
        out = jnp.where(lane == i, value, out)
    return out


def row_sum(value):
    return jnp.sum(value, axis=1, keepdims=True)


def cost(rows):
    return pl.CostEstimate(flops=6 * rows * IFACE * IFACE, bytes_accessed=8 << 20, transcendentals=0)


def call(body, outs, n_in, name, smem=(), scratch=(), estimate=None, grant=2):
    return pl.pallas_call(
        body,
        out_shape=tuple(jax.ShapeDtypeStruct(s, F32) for s in outs),
        in_specs=[SMEM if i in smem else VMEM for i in range(n_in)],
        out_specs=tuple(VMEM for _ in outs),
        scratch_shapes=list(scratch),
        compiler_params=pltpu.CompilerParams(vmem_limit_bytes=grant << 20),
        cost_estimate=estimate,
        name=name,
    )


def times_matrix(u_high, u_low, matrix_ref, store):
    for i in range(4):
        store(i, product((u_high[...], u_low[...]), parts(quarter(matrix_ref, i))))


def keep(u_high, u_low, i, value):
    high, low = parts(value)
    u_high[:, i * FACE : (i + 1) * FACE] = high
    u_low[:, i * FACE : (i + 1) * FACE] = low


U_SCRATCH = (pltpu.VMEM((CASES, IFACE), BF16), pltpu.VMEM((CASES, IFACE), BF16))


def position():
    span = lax.axis_index("z") * Y + lax.axis_index("y")
    return span, lax.axis_index("x") * 2 + lax.axis_index("core")


def live_row(ref, on):
    block = lax.broadcasted_iota(jnp.int32, (1, FACE), 1) // (FACE // GB)
    row = jnp.zeros((1, FACE), F32)
    for b in range(GB):
        row = jnp.where(block == b, ref[b].astype(F32), row)
    return row * on.astype(F32)


def faces_times(first, third, matrix, rows, i):
    at = slice(i * FACE, (i + 1) * FACE)
    return product(first, parts(matrix[rows : rows + FACE, at])) + product(
        third, parts(matrix[rows + 2 * FACE : rows + 3 * FACE, at])
    )


def own_kernel(active, deck, joint, matrix, part):
    span, across = position()
    first = parts((across < DECKS - 1).astype(F32) * deck[...])
    third = parts(live_row(active, span < SPANS - 1) * joint[...])
    for i in range(4):
        part[:, i * FACE : (i + 1) * FACE] = faces_times(first, third, matrix, 0, i)


def behind_kernel(active, active_behind, deck_behind, joint_behind, part, matrix,
                  v0, v1, v2, v3, masks):
    span, across = position()
    ones = jnp.ones((1, FACE), F32)
    lives = (
        ones * (across < DECKS - 1).astype(F32),
        ones * (across > 0).astype(F32),
        live_row(active, span < SPANS - 1),
        live_row(active_behind, span > 0),
    )
    masks[...] = jnp.concatenate(lives + (jnp.zeros((4, FACE), F32),), axis=0)
    second, fourth = parts(lives[1] * deck_behind[...]), parts(lives[3] * joint_behind[...])
    for i, out in enumerate((v0, v1, v2, v3)):
        out[...] = 0.5 * (quarter(part, i) - faces_times(second, fourth, matrix, FACE, i))


def jump(masks, own, got, i):
    return masks[i : i + 1, :] * (own[i][: CASES, :] - got[i][: CASES, :])


def flex_kernel(n_faces, masks, f0, f1, f2, f3, g0, g1, g2, g3, matrix, corners, *refs):
    pairs, refs = refs[: 2 * n_faces], refs[2 * n_faces :]
    outs, (first, third, sent, held, u_high, u_low, u_full, table) = refs[:4], refs[4:]
    core = lax.axis_index("core")
    own, got = (f0, f1, f2, f3), (g0, g1, g2, g3)
    for i in range(4):
        value = jump(masks, own, got, i)
        keep(u_high, u_low, i, value)
        u_full[:, i * FACE : (i + 1) * FACE] = value
    first[...] = quarter(u_full, 0)
    third[...] = quarter(u_full, 2)
    total = jnp.zeros((CASES, 1), F32)
    for i in range(4):
        value = product((u_high[...], u_low[...]), parts(quarter(matrix, i)))
        total = total + row_sum(quarter(u_full, i) * value)
        if outs[i].shape[0] == CASES:
            outs[i][...] = value
        else:
            outs[i][: CASES, :] = value
            outs[i][CASES:, :] = quarter(corners, i)
    sums = [
        row_sum(masks[0:1, :] * pairs[2 * k][...] * first[...] + masks[2:3, :] * pairs[2 * k + 1][...] * third[...])
        for k in range(n_faces)
    ]
    table[:, :NC] = product((u_high[...], u_low[...]), parts(corners[...]), TRANS)
    lane = lax.broadcasted_iota(jnp.int32, (CASES, 128), 1)
    table[:, NC:] = column(lane, total, *sums)
    held[...] = table[pl.ds(pl.multiple_of(core * HALF, HALF), HALF), :]
    sent[...] = table[pl.ds(pl.multiple_of((1 - core) * HALF, HALF), HALF), :]


def total_of(got):
    part = got[0]
    for k in range(1, Z):
        part = part + got[k]
    return part


def first_coarse_kernel(got, coarse, out, scalars):
    part = total_of(got)
    total = part[:, :NC]
    load = SCALE * product(parts(total), parts(coarse[...]))
    curv = part[:, NC : NC + 1] + row_sum(load * total)
    rz = part[:, NC + 1 : NC + 2]
    lane = lax.broadcasted_iota(jnp.int32, (PIECE, 128), 1)
    row = jnp.concatenate([load, column(lane, rz / curv)], axis=1)
    for k in range(Y * X):
        out[k] = row
    scalars[...] = column(lane, rz, curv)


def second_coarse_kernel(got, coarse, scalars, out):
    part = total_of(got)
    total = part[:, :NC]
    load = SCALE * product(parts(total), parts(coarse[...]))
    own = part[:, NC : NC + 1] + row_sum(load * total)
    new = part[:, NC + 1 : NC + 2]
    cross = part[:, NC + 2 : NC + 3]
    rz, curv = scalars[:, 0:1], scalars[:, 1:2]
    ratio = new / rz
    second = new / (own + ratio * (2.0 * cross + ratio * curv))
    lane = lax.broadcasted_iota(jnp.int32, (PIECE, 128), 1)
    row = jnp.concatenate([second * load, column(lane, second, second * ratio)], axis=1)
    for k in range(Y * X):
        out[k] = row


def place_rows(mine, other, whole):
    core = lax.axis_index("core")
    whole[pl.ds(pl.multiple_of(core * HALF, HALF), HALF), :] = mine[...]
    whole[pl.ds(pl.multiple_of((1 - core) * HALF, HALF), HALF), :] = other[...]


def precond_kernel(masks, mine, other, f0, f1, f2, f3, g0, g1, g2, g3,
                   deck, joint, deck_behind, joint_behind, matrix,
                   v0, v1, v2, v3, image_deck, image_joint, res_deck, res_joint,
                   corner_deck, corner_joint, steps, u_high, u_low, whole):
    place_rows(mine, other, whole)
    load = parts(whole[:, :NC])
    step = whole[:, NC : NC + 1]
    steps[...] = whole[:, NC:]
    own, got = (f0, f1, f2, f3), (g0, g1, g2, g3)
    gaps = (deck, deck_behind, joint, joint_behind)
    for i in range(4):
        live = masks[i : i + 1, :]
        corner = live * (own[i][CASES:, :] - got[i][CASES:, :])
        image = jump(masks, own, got, i) + product(load, parts(corner))
        gap = live * gaps[i][...]
        res = (gap if i % 2 == 0 else -gap) - step * image
        if i == 0:
            corner_deck[...], image_deck[...], res_deck[...] = corner, image, res
        if i == 2:
            corner_joint[...], image_joint[...], res_joint[...] = corner, image, res
        keep(u_high, u_low, i, res)

    def store(i, value):
        (v0, v1, v2, v3)[i][...] = 0.5 * value

    times_matrix(u_high, u_low, matrix, store)


def final_kernel(masks, mine, other, steps, z_deck, z_joint, y_deck, y_joint,
                 image_deck, image_joint, res_deck, res_joint, corner_deck, corner_joint,
                 f0, f2, g0, g2, sol_deck, sol_joint, out_deck, out_joint, whole):
    place_rows(mine, other, whole)
    load = parts(whole[:, :NC])
    second, mixed = whole[:, NC : NC + 1], whole[:, NC + 1 : NC + 2]
    first = steps[:, 0:1] + mixed
    sol_deck[...] = first * z_deck[...] + second * y_deck[...]
    sol_joint[...] = first * z_joint[...] + second * y_joint[...]
    for i, res, field, ahead, image, corner, out in (
        (0, res_deck, f0, g0, image_deck, corner_deck, out_deck),
        (2, res_joint, f2, g2, image_joint, corner_joint, out_joint),
    ):
        reaction = masks[i : i + 1, :] * (field[...] - ahead[...])
        out[...] = (
            res[...] - second * reaction - mixed * image[...] - product(load, parts(corner[...]))
        )


def exchange(field):
    right, left, ahead, behind = field
    ahead_got, behind_got = cyclic(ahead, SPAN, 1), cyclic(behind, SPAN, -1)
    right_got, left_got = cyclic(right, DECK, 1), cyclic(left, DECK, -1)
    return left_got, right_got, behind_got, ahead_got


def add_kernel(held, got, out):
    for k in range(Y * X):
        at = slice(k * PIECE, (k + 1) * PIECE)
        out[k] = held[at, :] + got[at, :]


def spread_kernel(got, out):
    part = got[0]
    for k in range(1, Y * X):
        part = part + got[k]
    for k in range(Z):
        out[k] = part


def reduce_rows(sent, held):
    (block,) = call(add_kernel, [(Y * X, PIECE, WIDE)], 2, "add")(held, swapped(sent))
    got = lax.all_to_all(block, ("y", "x"), 0, 0)
    (copies,) = call(spread_kernel, [(Z, PIECE, WIDE)], 1, "spread")(got)
    return lax.all_to_all(copies, "z", 0, 0)


def gather_rows(copies):
    mine = lax.all_to_all(copies, ("y", "x"), 0, 0).reshape(HALF, WIDE)
    return mine, swapped(mine)


def after(values, *others):
    return lax.optimization_barrier((values, others))[0]


def local(flex, precond, corner_map, coarse_inverse, gap_deck, gap_joint, active):
    flex, precond, corners = flex[0, 0], precond[0, 0], corner_map[0, 0]
    deck, joint, active = gap_deck[0, 0], gap_joint[0, 0], active[0, 0]
    face, field, stacked = (CASES, FACE), [(CASES, FACE)] * 4, [(2 * CASES, FACE)] * 4
    half, copies = (HALF, WIDE), (Y * X, PIECE, WIDE)
    full = pltpu.VMEM((CASES, IFACE), F32)
    whole = pltpu.VMEM((CASES, WIDE), F32)

    joint_behind = cyclic(joint, SPAN, 1)
    deck_behind = cyclic(deck, DECK, 1)
    active_behind = cyclic(active, SPAN, 1)
    gaps = (deck, joint, deck_behind, joint_behind)
    (part,) = call(
        own_kernel, [(CASES, IFACE)], 4, "own", smem=(0,), estimate=cost(CASES // 2), grant=10
    )(active, deck, joint, precond)
    *v, masks = call(
        behind_kernel, field + [(8, FACE)], 6, "behind", smem=(0, 1), estimate=cost(CASES // 2), grant=10
    )(active, active_behind, deck_behind, joint_behind, part, precond)
    *w, z_deck, z_joint, sent, held = call(
        functools.partial(flex_kernel, 1), stacked + [face, face, half, half], 13, "flex_first",
        scratch=U_SCRATCH + (full, whole), estimate=cost(CASES), grant=10,
    )(masks, *v, *exchange(v), flex, corners, deck, joint)
    got = exchange(w)
    sums = reduce_rows(sent, held)
    loads, scalars = call(first_coarse_kernel, [copies, (PIECE, 128)], 2, "coarse_first")(
        sums, coarse_inverse
    )
    loads = after(loads, got)
    *v, image_deck, image_joint, res_deck, res_joint, corner_deck, corner_joint, steps = call(
        precond_kernel, field + [face] * 6 + [(CASES, 128)], 16, "precond",
        scratch=U_SCRATCH + (whole,), estimate=cost(CASES), grant=10,
    )(masks, *gather_rows(loads), *w, *got, *gaps, precond)
    *w, y_deck, y_joint, sent, held = call(
        functools.partial(flex_kernel, 2), field + [face, face, half, half], 15, "flex_second",
        scratch=U_SCRATCH + (full, whole), estimate=cost(CASES), grant=10,
    )(masks, *v, *exchange(v), flex, corners, res_deck, res_joint, image_deck, image_joint)
    got = cyclic(w[1], DECK, -1), cyclic(w[3], SPAN, -1)
    sums = reduce_rows(sent, held)
    (loads,) = call(second_coarse_kernel, [copies], 3, "coarse_second")(sums, coarse_inverse, scalars)
    loads = after(loads, got)
    outs = call(
        final_kernel, [face] * 4, 18, "final", scratch=(whole,), grant=6
    )(
        masks, *gather_rows(loads), steps, z_deck, z_joint, y_deck, y_joint,
        image_deck, image_joint, res_deck, res_joint, corner_deck, corner_joint, w[0], w[2], *got,
    )
    return tuple(out[None, None] for out in outs)


def solution(mesh):
    mesh = Mesh(mesh.devices.reshape(Z, Y, X, 2), SPAN + DECK)
    block = P(SPAN, DECK, None, None)
    in_specs = (block, block, block, P(), block, block, P(SPAN, DECK, None))
    return jax.shard_map(
        local, mesh=mesh, in_specs=in_specs, out_specs=(block,) * 4, check_vma=False
    )
```

```python
import functools
import math

import jax
import jax.numpy as jnp
from jax import lax
from jax.experimental import pallas as pl
from jax.experimental.pallas import tpu as pltpu
from jax.sharding import Mesh
from jax.sharding import PartitionSpec as P

SPAN, DECK = ("z", "y"), ("x", "core")
SPANS, DECKS, Y, X, Z = 32, 8, 4, 4, 8
CASES, FACE, IFACE, NC, GB = 256, 256, 1024, 256, 4
WIDE = NC + 128
HALF = CASES // 2
PIECE = HALF // (Y * X)
SCALE = 1.0 / math.sqrt(SPANS * DECKS)
F32, BF16 = jnp.float32, jnp.bfloat16
VMEM = pl.BlockSpec(memory_space=pltpu.VMEM)
SMEM = pl.BlockSpec(memory_space=pltpu.SMEM)


def cyclic(block, axes, k):
    n = SPANS if axes == SPAN else DECKS
    return lax.ppermute(block, axes, [(i, (i + k) % n) for i in range(n)])


def swapped(block):
    return lax.ppermute(block, "core", [(0, 1), (1, 0)])


def parts(value):
    high = value.astype(BF16)
    return high, (value - high.astype(F32)).astype(BF16)


def product(left, right, dims=(((1,), (0,)), ((), ()))):
    dot = functools.partial(lax.dot_general, dimension_numbers=dims, preferred_element_type=F32)
    return dot(left[0], right[0]) + (dot(left[0], right[1]) + dot(left[1], right[0]))


TRANS = (((1,), (1,)), ((), ()))


def quarter(ref, i):
    return ref[:, i * FACE : (i + 1) * FACE]


def column(lane, *values):
    out = jnp.zeros((values[0].shape[0], 128), F32)
    for i, value in enumerate(values):
        out = jnp.where(lane == i, value, out)
    return out


def row_sum(value):
    return jnp.sum(value, axis=1, keepdims=True)


def cost(rows):
    return pl.CostEstimate(flops=6 * rows * IFACE * IFACE, bytes_accessed=8 << 20, transcendentals=0)


def call(body, outs, n_in, name, smem=(), scratch=(), estimate=None, grant=2):
    return pl.pallas_call(
        body,
        out_shape=tuple(s if isinstance(s, jax.ShapeDtypeStruct) else jax.ShapeDtypeStruct(s, F32) for s in outs),
        in_specs=[SMEM if i in smem else VMEM for i in range(n_in)],
        out_specs=tuple(VMEM for _ in outs),
        scratch_shapes=list(scratch),
        compiler_params=pltpu.CompilerParams(vmem_limit_bytes=grant << 20),
        cost_estimate=estimate,
        name=name,
    )


def keep(u_high, u_low, i, value):
    high, low = parts(value)
    u_high[:, i * FACE : (i + 1) * FACE] = high
    u_low[:, i * FACE : (i + 1) * FACE] = low


def position():
    span = lax.axis_index("z") * Y + lax.axis_index("y")
    return span, lax.axis_index("x") * 2 + lax.axis_index("core")


def live_row(ref, on):
    block = lax.broadcasted_iota(jnp.int32, (1, FACE), 1) // (FACE // GB)
    row = jnp.zeros((1, FACE), F32)
    for b in range(GB):
        row = jnp.where(block == b, ref[b].astype(F32), row)
    return row * on.astype(F32)


def faces_times(first, third, matrix, rows, i):
    at = slice(i * FACE, (i + 1) * FACE)
    return product(first, parts(matrix[rows : rows + FACE, at])) + product(
        third, parts(matrix[rows + 2 * FACE : rows + 3 * FACE, at])
    )


def own_kernel(active, deck, joint, matrix, part):
    span, across = position()
    first = parts((across < DECKS - 1).astype(F32) * deck[...])
    third = parts(live_row(active, span < SPANS - 1) * joint[...])
    for i in range(4):
        part[:, i * FACE : (i + 1) * FACE] = faces_times(first, third, matrix, 0, i)


def behind_kernel(which, active, active_behind, deck_behind, joint_behind, part, matrix, *outs):
    span, across = position()
    ones = jnp.ones((1, FACE), F32)
    lives = (
        ones * (across < DECKS - 1).astype(F32),
        ones * (across > 0).astype(F32),
        live_row(active, span < SPANS - 1),
        live_row(active_behind, span > 0),
    )
    if len(outs) == 3:
        outs[2][...] = jnp.concatenate(lives + (jnp.zeros((4, FACE), F32),), axis=0)
    second, fourth = parts(lives[1] * deck_behind[...]), parts(lives[3] * joint_behind[...])
    for i, out in zip(which, outs):
        out[...] = 0.5 * (quarter(part, i) - faces_times(second, fourth, matrix, FACE, i))


def jump(masks, own, got, i):
    return masks[i : i + 1, :] * (own[i][: CASES, :] - got[i][: CASES, :])


def two_quarters(masks, own, got, matrix, corners, at):
    jumps = [jump(masks, own, got, i) for i in range(2)]
    high, low = parts(jnp.concatenate(jumps, axis=1))
    rows = slice(at, at + 2 * FACE)
    fields = [product((high, low), parts(matrix[rows, i * FACE : (i + 1) * FACE])) for i in range(4)]
    return jumps, fields, product((high, low), parts(corners[:, rows]), TRANS)


def flex_span_kernel(masks, f2, f3, g2, g3, matrix, corners, part, corner_part):
    _, fields, corner = two_quarters(masks[2:4, :], (f2, f3), (g2, g3), matrix, corners, 2 * FACE)
    for i in range(4):
        part[:, i * FACE : (i + 1) * FACE] = fields[i]
    corner_part[...] = corner


def flex_kernel(n_faces, masks, f0, f1, f2, f3, g0, g1, g2, g3, part, corner_part, matrix, corners, *refs):
    pairs, refs = refs[: 2 * n_faces], refs[2 * n_faces :]
    outs, (first, third, sent, held, table) = refs[:4], refs[4:]
    core = lax.axis_index("core")
    late, fields, corner = two_quarters(masks[0:2, :], (f0, f1), (g0, g1), matrix, corners, 0)
    jumps = late + [jump(masks[2:4, :], (f2, f3), (g2, g3), i) for i in range(2)]
    first[...], third[...] = jumps[0], jumps[2]
    total = jnp.zeros((CASES, 1), F32)
    for i in range(4):
        value = quarter(part, i) + fields[i]
        total = total + row_sum(jumps[i] * value)
        if outs[i].shape[0] == CASES:
            outs[i][...] = value
        else:
            outs[i][: CASES, :] = value
            outs[i][CASES:, :] = quarter(corners, i)
    sums = [
        row_sum(masks[0:1, :] * pairs[2 * k][...] * first[...] + masks[2:3, :] * pairs[2 * k + 1][...] * third[...])
        for k in range(n_faces)
    ]
    table[:, :NC] = corner_part[...] + corner
    lane = lax.broadcasted_iota(jnp.int32, (CASES, 128), 1)
    table[:, NC:] = column(lane, total, *sums)
    held[...] = table[pl.ds(pl.multiple_of(core * HALF, HALF), HALF), :]
    sent[...] = table[pl.ds(pl.multiple_of((1 - core) * HALF, HALF), HALF), :]


def total_of(got):
    part = got[0]
    for k in range(1, Z):
        part = part + got[k]
    return part


def first_coarse_kernel(got, coarse, out, scalars):
    part = total_of(got)
    total = part[:, :NC]
    load = SCALE * product(parts(total), parts(coarse[...]))
    curv = part[:, NC : NC + 1] + row_sum(load * total)
    rz = part[:, NC + 1 : NC + 2]
    lane = lax.broadcasted_iota(jnp.int32, (PIECE, 128), 1)
    row = jnp.concatenate([load, column(lane, rz / curv)], axis=1)
    for k in range(Y * X):
        out[k] = row
    scalars[...] = column(lane, rz, curv)


def second_coarse_kernel(got, coarse, scalars, out):
    part = total_of(got)
    total = part[:, :NC]
    load = SCALE * product(parts(total), parts(coarse[...]))
    own = part[:, NC : NC + 1] + row_sum(load * total)
    new = part[:, NC + 1 : NC + 2]
    cross = part[:, NC + 2 : NC + 3]
    rz, curv = scalars[:, 0:1], scalars[:, 1:2]
    ratio = new / rz
    second = new / (own + ratio * (2.0 * cross + ratio * curv))
    lane = lax.broadcasted_iota(jnp.int32, (PIECE, 128), 1)
    row = jnp.concatenate([second * load, column(lane, second, second * ratio)], axis=1)
    for k in range(Y * X):
        out[k] = row


def place_rows(mine, other, whole):
    core = lax.axis_index("core")
    whole[pl.ds(pl.multiple_of(core * HALF, HALF), HALF), :] = mine[...]
    whole[pl.ds(pl.multiple_of((1 - core) * HALF, HALF), HALF), :] = other[...]


def precond_kernel(masks, mine, other, f0, f1, f2, f3, g0, g1, g2, g3,
                   deck, joint, deck_behind, joint_behind, matrix,
                   v2, v3, u_high, u_low, image_deck, image_joint, res_deck, res_joint,
                   corner_deck, corner_joint, steps, whole):
    place_rows(mine, other, whole)
    load = parts(whole[:, :NC])
    step = whole[:, NC : NC + 1]
    steps[...] = whole[:, NC:]
    own, got = (f0, f1, f2, f3), (g0, g1, g2, g3)
    gaps = (deck, deck_behind, joint, joint_behind)
    for i in range(4):
        live = masks[i : i + 1, :]
        corner = live * (own[i][CASES:, :] - got[i][CASES:, :])
        image = jump(masks, own, got, i) + product(load, parts(corner))
        gap = live * gaps[i][...]
        res = (gap if i % 2 == 0 else -gap) - step * image
        if i == 0:
            corner_deck[...], image_deck[...], res_deck[...] = corner, image, res
        if i == 2:
            corner_joint[...], image_joint[...], res_joint[...] = corner, image, res
        keep(u_high, u_low, i, res)

    span_quarters(u_high, u_low, matrix, v2, v3)


def two_of(first, u_high, u_low, matrix, outs):
    for i, out in enumerate(outs):
        out[...] = 0.5 * product((u_high[...], u_low[...]), parts(quarter(matrix, first + i)))


def span_quarters(u_high, u_low, matrix, v2, v3):
    two_of(2, u_high, u_low, matrix, (v2, v3))


def deck_quarters(u_high, u_low, matrix, v0, v1):
    two_of(0, u_high, u_low, matrix, (v0, v1))


def final_kernel(masks, mine, other, steps, z_deck, z_joint, y_deck, y_joint,
                 image_deck, image_joint, res_deck, res_joint, corner_deck, corner_joint,
                 f0, f2, g0, g2, sol_deck, sol_joint, out_deck, out_joint, whole):
    place_rows(mine, other, whole)
    load = parts(whole[:, :NC])
    second, mixed = whole[:, NC : NC + 1], whole[:, NC + 1 : NC + 2]
    first = steps[:, 0:1] + mixed
    sol_deck[...] = first * z_deck[...] + second * y_deck[...]
    sol_joint[...] = first * z_joint[...] + second * y_joint[...]
    for i, res, field, ahead, image, corner, out in (
        (0, res_deck, f0, g0, image_deck, corner_deck, out_deck),
        (2, res_joint, f2, g2, image_joint, corner_joint, out_joint),
    ):
        reaction = masks[i : i + 1, :] * (field[...] - ahead[...])
        out[...] = (
            res[...] - second * reaction - mixed * image[...] - product(load, parts(corner[...]))
        )


def exchange(field):
    right, left, ahead, behind = field
    ahead_got, behind_got = cyclic(ahead, SPAN, 1), cyclic(behind, SPAN, -1)
    right_got, left_got = cyclic(right, DECK, 1), cyclic(left, DECK, -1)
    return left_got, right_got, behind_got, ahead_got


def add_kernel(held, got, out):
    for k in range(Y * X):
        at = slice(k * PIECE, (k + 1) * PIECE)
        out[k] = held[at, :] + got[at, :]


def spread_kernel(got, out):
    part = got[0]
    for k in range(1, Y * X):
        part = part + got[k]
    for k in range(Z):
        out[k] = part


def scatter_rows(sent, held):
    (block,) = call(add_kernel, [(Y * X, PIECE, WIDE)], 2, "add")(held, swapped(sent))
    return lax.all_to_all(block, ("y", "x"), 0, 0)


def along_z(got):
    (copies,) = call(spread_kernel, [(Z, PIECE, WIDE)], 1, "spread")(got)
    return lax.all_to_all(copies, "z", 0, 0)


def gather_rows(copies):
    mine = lax.all_to_all(copies, ("y", "x"), 0, 0).reshape(HALF, WIDE)
    return mine, swapped(mine)


def after(values, *others):
    return lax.optimization_barrier((values, others))[0]


def local(flex, precond, corner_map, coarse_inverse, gap_deck, gap_joint, active):
    flex, precond, corners = flex[0, 0], precond[0, 0], corner_map[0, 0]
    deck, joint, active = gap_deck[0, 0], gap_joint[0, 0], active[0, 0]
    face, pair, field, stacked = (CASES, FACE), [(CASES, FACE)] * 2, [(CASES, FACE)] * 4, [(2 * CASES, FACE)] * 4
    wide, half, copies = (CASES, IFACE), (HALF, WIDE), (Y * X, PIECE, WIDE)
    narrow = [jax.ShapeDtypeStruct(wide, BF16)] * 2
    whole = pltpu.VMEM((CASES, WIDE), F32)

    def flexed(n_faces, v, name, shapes, *pairs):
        got = exchange(v)
        part, corner = call(
            flex_span_kernel, [wide, (CASES, NC)], 7, name + "_span", estimate=cost(CASES // 2), grant=10
        )(masks, *v[2:], *got[2:], flex, corners)
        return call(
            functools.partial(flex_kernel, n_faces), shapes + [face, face, half, half], 13 + 2 * n_faces,
            name, scratch=(whole,), estimate=cost(CASES // 2), grant=10,
        )(masks, *v, *got, part, corner, flex, corners, *pairs)

    joint_behind = cyclic(joint, SPAN, 1)
    deck_behind = cyclic(deck, DECK, 1)
    active_behind = cyclic(active, SPAN, 1)
    gaps = (deck, joint, deck_behind, joint_behind)
    (part,) = call(
        own_kernel, [wide], 4, "own", smem=(0,), estimate=cost(CASES // 2), grant=10
    )(active, deck, joint, precond)
    behind = (active, active_behind, deck_behind, joint_behind, part, precond)
    v2, v3, masks = call(
        functools.partial(behind_kernel, (2, 3)), pair + [(8, FACE)], 6, "behind_span",
        smem=(0, 1), estimate=cost(CASES // 4), grant=10,
    )(*behind)
    v0, v1 = call(
        functools.partial(behind_kernel, (0, 1)), pair, 6, "behind_deck",
        smem=(0, 1), estimate=cost(CASES // 4), grant=10,
    )(*behind)
    *w, z_deck, z_joint, sent, held = flexed(1, (v0, v1, v2, v3), "flex_first", stacked, deck, joint)
    rows = scatter_rows(sent, held)
    got = exchange(after(w, rows))
    loads, scalars = call(first_coarse_kernel, [copies, (PIECE, 128)], 2, "coarse_first")(
        along_z(rows), coarse_inverse
    )
    loads = after(loads, got)
    v2, v3, *u, image_deck, image_joint, res_deck, res_joint, corner_deck, corner_joint, steps = call(
        precond_kernel, pair + narrow + [face] * 6 + [(CASES, 128)], 16, "precond_span",
        scratch=(whole,), estimate=cost(CASES // 2), grant=10,
    )(masks, *gather_rows(loads), *w, *got, *gaps, precond)
    v0, v1 = call(
        deck_quarters, pair, 3, "precond_deck", estimate=cost(CASES // 2), grant=10
    )(*u, precond)
    *w, y_deck, y_joint, sent, held = flexed(
        2, (v0, v1, v2, v3), "flex_second", field, res_deck, res_joint, image_deck, image_joint
    )
    rows = scatter_rows(sent, held)
    left, behind = after((w[1], w[3]), rows)
    got = cyclic(left, DECK, -1), cyclic(behind, SPAN, -1)
    (loads,) = call(second_coarse_kernel, [copies], 3, "coarse_second")(
        along_z(rows), coarse_inverse, scalars
    )
    loads = after(loads, got)
    outs = call(
        final_kernel, [face] * 4, 18, "final", scratch=(whole,), grant=6
    )(
        masks, *gather_rows(loads), steps, z_deck, z_joint, y_deck, y_joint,
        image_deck, image_joint, res_deck, res_joint, corner_deck, corner_joint, w[0], w[2], *got,
    )
    return tuple(out[None, None] for out in outs)


def solution(mesh):
    mesh = Mesh(mesh.devices.reshape(Z, Y, X, 2), SPAN + DECK)
    block = P(SPAN, DECK, None, None)
    in_specs = (block, block, block, P(), block, block, P(SPAN, DECK, None))
    return jax.shard_map(
        local, mesh=mesh, in_specs=in_specs, out_specs=(block,) * 4, check_vma=False
    )
```

```python
import functools
import math

import jax
import jax.numpy as jnp
from jax import lax
from jax.experimental import pallas as pl
from jax.experimental.pallas import tpu as pltpu
from jax.sharding import Mesh
from jax.sharding import PartitionSpec as P

SPAN, DECK = ("z", "y"), ("x", "core")
SPANS, DECKS, Y, X, Z = 32, 8, 4, 4, 8
CASES, FACE, IFACE, NC, GB = 256, 256, 1024, 256, 4
WIDE = NC + 128
HALF = CASES // 2
PIECE = HALF // (Y * X)
SCALE = 1.0 / math.sqrt(SPANS * DECKS)
F32, BF16 = jnp.float32, jnp.bfloat16
VMEM = pl.BlockSpec(memory_space=pltpu.VMEM)
SMEM = pl.BlockSpec(memory_space=pltpu.SMEM)


def cyclic(block, axes, k):
    n = SPANS if axes == SPAN else DECKS
    return lax.ppermute(block, axes, [(i, (i + k) % n) for i in range(n)])


def swapped(block):
    return lax.ppermute(block, "core", [(0, 1), (1, 0)])


def parts(value):
    high = value.astype(BF16)
    return high, (value - high.astype(F32)).astype(BF16)


def product(left, right, dims=(((1,), (0,)), ((), ()))):
    dot = functools.partial(lax.dot_general, dimension_numbers=dims, preferred_element_type=F32)
    return dot(left[0], right[0]) + (dot(left[0], right[1]) + dot(left[1], right[0]))


TRANS = (((1,), (1,)), ((), ()))


def quarter(ref, i):
    return ref[:, i * FACE : (i + 1) * FACE]


def column(lane, *values):
    out = jnp.zeros((values[0].shape[0], 128), F32)
    for i, value in enumerate(values):
        out = jnp.where(lane == i, value, out)
    return out


def row_sum(value):
    return jnp.sum(value, axis=1, keepdims=True)


def cost(rows):
    return pl.CostEstimate(flops=6 * rows * IFACE * IFACE, bytes_accessed=8 << 20, transcendentals=0)


def call(body, outs, n_in, name, smem=(), scratch=(), estimate=None, grant=2):
    return pl.pallas_call(
        body,
        out_shape=tuple(s if isinstance(s, jax.ShapeDtypeStruct) else jax.ShapeDtypeStruct(s, F32) for s in outs),
        in_specs=[SMEM if i in smem else VMEM for i in range(n_in)],
        out_specs=tuple(VMEM for _ in outs),
        scratch_shapes=list(scratch),
        compiler_params=pltpu.CompilerParams(vmem_limit_bytes=grant << 20),
        cost_estimate=estimate,
        name=name,
    )


def keep(u_high, u_low, i, value):
    high, low = parts(value)
    u_high[:, i * FACE : (i + 1) * FACE] = high
    u_low[:, i * FACE : (i + 1) * FACE] = low


def position():
    span = lax.axis_index("z") * Y + lax.axis_index("y")
    return span, lax.axis_index("x") * 2 + lax.axis_index("core")


def live_row(ref, on):
    block = lax.broadcasted_iota(jnp.int32, (1, FACE), 1) // (FACE // GB)
    row = jnp.zeros((1, FACE), F32)
    for b in range(GB):
        row = jnp.where(block == b, ref[b].astype(F32), row)
    return row * on.astype(F32)


def faces_times(first, third, matrix, rows, i):
    at = slice(i * FACE, (i + 1) * FACE)
    return product(first, parts(matrix[rows : rows + FACE, at])) + product(
        third, parts(matrix[rows + 2 * FACE : rows + 3 * FACE, at])
    )


def lives_kernel(active, out):
    out[...] = jnp.broadcast_to(live_row(active, position()[0] < SPANS - 1), (8, FACE))


def own_kernel(lives, deck, joint, matrix, part):
    first = parts((position()[1] < DECKS - 1).astype(F32) * deck[...])
    third = parts(lives[0:1, :] * joint[...])
    for i in range(4):
        part[:, i * FACE : (i + 1) * FACE] = faces_times(first, third, matrix, 0, i)


def behind_kernel(which, active, active_behind, deck_behind, joint_behind, part, matrix, *outs):
    span, across = position()
    ones = jnp.ones((1, FACE), F32)
    lives = (
        ones * (across < DECKS - 1).astype(F32),
        ones * (across > 0).astype(F32),
        live_row(active, span < SPANS - 1),
        live_row(active_behind, span > 0),
    )
    if len(outs) == 3:
        outs[2][...] = jnp.concatenate(lives + (jnp.zeros((4, FACE), F32),), axis=0)
    second, fourth = parts(lives[1] * deck_behind[...]), parts(lives[3] * joint_behind[...])
    for i, out in zip(which, outs):
        out[...] = 0.5 * (quarter(part, i) - faces_times(second, fourth, matrix, FACE, i))


def jump(masks, own, got, i):
    return masks[i : i + 1, :] * (own[i][: CASES, :] - got[i][: CASES, :])


def two_quarters(masks, own, got, matrix, corners, at):
    jumps = [jump(masks, own, got, i) for i in range(2)]
    high, low = parts(jnp.concatenate(jumps, axis=1))
    rows = slice(at, at + 2 * FACE)
    fields = [product((high, low), parts(matrix[rows, i * FACE : (i + 1) * FACE])) for i in range(4)]
    return jumps, fields, product((high, low), parts(corners[:, rows]), TRANS)


def flex_span_kernel(masks, f2, f3, g2, g3, matrix, corners, part, corner_part):
    _, fields, corner = two_quarters(masks[2:4, :], (f2, f3), (g2, g3), matrix, corners, 2 * FACE)
    for i in range(4):
        part[:, i * FACE : (i + 1) * FACE] = fields[i]
    corner_part[...] = corner


def flex_kernel(n_faces, masks, f0, f1, f2, f3, g0, g1, g2, g3, part, corner_part, matrix, corners, *refs):
    pairs, refs = refs[: 2 * n_faces], refs[2 * n_faces :]
    outs, (first, third, sent, held, table) = refs[:4], refs[4:]
    core = lax.axis_index("core")
    late, fields, corner = two_quarters(masks[0:2, :], (f0, f1), (g0, g1), matrix, corners, 0)
    jumps = late + [jump(masks[2:4, :], (f2, f3), (g2, g3), i) for i in range(2)]
    first[...], third[...] = jumps[0], jumps[2]
    total = jnp.zeros((CASES, 1), F32)
    for i in range(4):
        value = quarter(part, i) + fields[i]
        total = total + row_sum(jumps[i] * value)
        if outs[i].shape[0] == CASES:
            outs[i][...] = value
        else:
            outs[i][: CASES, :] = value
            outs[i][CASES:, :] = quarter(corners, i)
    sums = [
        row_sum(masks[0:1, :] * pairs[2 * k][...] * first[...] + masks[2:3, :] * pairs[2 * k + 1][...] * third[...])
        for k in range(n_faces)
    ]
    table[:, :NC] = corner_part[...] + corner
    lane = lax.broadcasted_iota(jnp.int32, (CASES, 128), 1)
    table[:, NC:] = column(lane, total, *sums)
    held[...] = table[pl.ds(pl.multiple_of(core * HALF, HALF), HALF), :]
    sent[...] = table[pl.ds(pl.multiple_of((1 - core) * HALF, HALF), HALF), :]


def total_of(got):
    part = got[0]
    for k in range(1, Z):
        part = part + got[k]
    return part


def first_coarse_kernel(got, coarse, out, scalars):
    part = total_of(got)
    total = part[:, :NC]
    load = SCALE * product(parts(total), parts(coarse[...]))
    curv = part[:, NC : NC + 1] + row_sum(load * total)
    rz = part[:, NC + 1 : NC + 2]
    lane = lax.broadcasted_iota(jnp.int32, (PIECE, 128), 1)
    row = jnp.concatenate([load, column(lane, rz / curv)], axis=1)
    for k in range(Y * X):
        out[k] = row
    scalars[...] = column(lane, rz, curv)


def second_coarse_kernel(got, coarse, scalars, out):
    part = total_of(got)
    total = part[:, :NC]
    load = SCALE * product(parts(total), parts(coarse[...]))
    own = part[:, NC : NC + 1] + row_sum(load * total)
    new = part[:, NC + 1 : NC + 2]
    cross = part[:, NC + 2 : NC + 3]
    rz, curv = scalars[:, 0:1], scalars[:, 1:2]
    ratio = new / rz
    second = new / (own + ratio * (2.0 * cross + ratio * curv))
    lane = lax.broadcasted_iota(jnp.int32, (PIECE, 128), 1)
    row = jnp.concatenate([second * load, column(lane, second, second * ratio)], axis=1)
    for k in range(Y * X):
        out[k] = row


def place_rows(mine, other, whole):
    core = lax.axis_index("core")
    whole[pl.ds(pl.multiple_of(core * HALF, HALF), HALF), :] = mine[...]
    whole[pl.ds(pl.multiple_of((1 - core) * HALF, HALF), HALF), :] = other[...]


def precond_kernel(masks, mine, other, f0, f1, f2, f3, g0, g1, g2, g3,
                   deck, joint, deck_behind, joint_behind, matrix,
                   v2, v3, u_high, u_low, image_deck, image_joint, res_deck, res_joint,
                   corner_deck, corner_joint, steps, whole):
    place_rows(mine, other, whole)
    load = parts(whole[:, :NC])
    step = whole[:, NC : NC + 1]
    steps[...] = whole[:, NC:]
    own, got = (f0, f1, f2, f3), (g0, g1, g2, g3)
    gaps = (deck, deck_behind, joint, joint_behind)
    for i in range(4):
        live = masks[i : i + 1, :]
        corner = live * (own[i][CASES:, :] - got[i][CASES:, :])
        image = jump(masks, own, got, i) + product(load, parts(corner))
        gap = live * gaps[i][...]
        res = (gap if i % 2 == 0 else -gap) - step * image
        if i == 0:
            corner_deck[...], image_deck[...], res_deck[...] = corner, image, res
        if i == 2:
            corner_joint[...], image_joint[...], res_joint[...] = corner, image, res
        keep(u_high, u_low, i, res)

    span_quarters(u_high, u_low, matrix, v2, v3)


def two_of(first, u_high, u_low, matrix, outs):
    for i, out in enumerate(outs):
        out[...] = 0.5 * product((u_high[...], u_low[...]), parts(quarter(matrix, first + i)))


def span_quarters(u_high, u_low, matrix, v2, v3):
    two_of(2, u_high, u_low, matrix, (v2, v3))


def deck_quarters(u_high, u_low, matrix, v0, v1):
    two_of(0, u_high, u_low, matrix, (v0, v1))


def final_kernel(masks, mine, other, steps, z_deck, z_joint, y_deck, y_joint,
                 image_deck, image_joint, res_deck, res_joint, corner_deck, corner_joint,
                 f0, f2, g0, g2, sol_deck, sol_joint, out_deck, out_joint, whole):
    place_rows(mine, other, whole)
    load = parts(whole[:, :NC])
    second, mixed = whole[:, NC : NC + 1], whole[:, NC + 1 : NC + 2]
    first = steps[:, 0:1] + mixed
    sol_deck[...] = first * z_deck[...] + second * y_deck[...]
    sol_joint[...] = first * z_joint[...] + second * y_joint[...]
    for i, res, field, ahead, image, corner, out in (
        (0, res_deck, f0, g0, image_deck, corner_deck, out_deck),
        (2, res_joint, f2, g2, image_joint, corner_joint, out_joint),
    ):
        reaction = masks[i : i + 1, :] * (field[...] - ahead[...])
        out[...] = (
            res[...] - second * reaction - mixed * image[...] - product(load, parts(corner[...]))
        )


def exchange(field):
    right, left, ahead, behind = field
    ahead_got, behind_got = cyclic(ahead, SPAN, 1), cyclic(behind, SPAN, -1)
    right_got, left_got = cyclic(right, DECK, 1), cyclic(left, DECK, -1)
    return left_got, right_got, behind_got, ahead_got


def add_kernel(held, got, out):
    for k in range(Y * X):
        at = slice(k * PIECE, (k + 1) * PIECE)
        out[k] = held[at, :] + got[at, :]


def spread_kernel(got, out):
    part = got[0]
    for k in range(1, Y * X):
        part = part + got[k]
    for k in range(Z):
        out[k] = part


def scatter_rows(sent, held):
    (block,) = call(add_kernel, [(Y * X, PIECE, WIDE)], 2, "add")(held, swapped(sent))
    return lax.all_to_all(block, ("y", "x"), 0, 0)


def along_z(got):
    (copies,) = call(spread_kernel, [(Z, PIECE, WIDE)], 1, "spread")(got)
    return lax.all_to_all(copies, "z", 0, 0)


def gather_rows(copies):
    mine = lax.all_to_all(copies, ("y", "x"), 0, 0).reshape(HALF, WIDE)
    return mine, swapped(mine)


def after(values, *others):
    return lax.optimization_barrier((values, others))[0]


def local(flex, precond, corner_map, coarse_inverse, gap_deck, gap_joint, active):
    flex, precond, corners = flex[0, 0], precond[0, 0], corner_map[0, 0]
    deck, joint, active = gap_deck[0, 0], gap_joint[0, 0], active[0, 0]
    face, pair, field, stacked = (CASES, FACE), [(CASES, FACE)] * 2, [(CASES, FACE)] * 4, [(2 * CASES, FACE)] * 4
    wide, half, copies = (CASES, IFACE), (HALF, WIDE), (Y * X, PIECE, WIDE)
    narrow = [jax.ShapeDtypeStruct(wide, BF16)] * 2
    whole = pltpu.VMEM((CASES, WIDE), F32)

    def flexed(n_faces, v, name, shapes, *pairs):
        got = exchange(v)
        part, corner = call(
            flex_span_kernel, [wide, (CASES, NC)], 7, name + "_span", estimate=cost(CASES // 2), grant=10
        )(masks, *v[2:], *got[2:], flex, corners)
        return call(
            functools.partial(flex_kernel, n_faces), shapes + [face, face, half, half], 13 + 2 * n_faces,
            name, scratch=(whole,), estimate=cost(CASES // 2), grant=10,
        )(masks, *v, *got, part, corner, flex, corners, *pairs)

    joint_behind = cyclic(joint, SPAN, 1)
    deck_behind = cyclic(deck, DECK, 1)
    active_behind = cyclic(active, SPAN, 1)
    gaps = (deck, joint, deck_behind, joint_behind)
    (lives,) = call(lives_kernel, [(8, FACE)], 1, "lives", smem=(0,), estimate=cost(4 * CASES))(active)
    (part,) = call(
        own_kernel, [wide], 4, "own", estimate=cost(CASES // 2), grant=10
    )(lives, deck, joint, precond)
    behind = (active, active_behind, deck_behind, joint_behind, part, precond)
    v2, v3, masks = call(
        functools.partial(behind_kernel, (2, 3)), pair + [(8, FACE)], 6, "behind_span",
        smem=(0, 1), estimate=cost(CASES // 4), grant=10,
    )(*behind)
    v0, v1 = call(
        functools.partial(behind_kernel, (0, 1)), pair, 6, "behind_deck",
        smem=(0, 1), estimate=cost(CASES // 4), grant=10,
    )(*behind)
    *w, z_deck, z_joint, sent, held = flexed(1, (v0, v1, v2, v3), "flex_first", stacked, deck, joint)
    rows = scatter_rows(sent, held)
    loads, scalars = call(first_coarse_kernel, [copies, (PIECE, 128)], 2, "coarse_first")(
        along_z(rows), coarse_inverse
    )
    got = exchange(after(w, loads))
    v2, v3, *u, image_deck, image_joint, res_deck, res_joint, corner_deck, corner_joint, steps = call(
        precond_kernel, pair + narrow + [face] * 6 + [(CASES, 128)], 16, "precond_span",
        scratch=(whole,), estimate=cost(CASES // 2), grant=10,
    )(masks, *gather_rows(loads), *w, *got, *gaps, precond)
    v0, v1 = call(
        deck_quarters, pair, 3, "precond_deck", estimate=cost(CASES // 2), grant=10
    )(*u, precond)
    *w, y_deck, y_joint, sent, held = flexed(
        2, (v0, v1, v2, v3), "flex_second", field, res_deck, res_joint, image_deck, image_joint
    )
    rows = scatter_rows(sent, held)
    left, behind = after((w[1], w[3]), rows)
    got = cyclic(left, DECK, -1), cyclic(behind, SPAN, -1)
    (loads,) = call(second_coarse_kernel, [copies], 3, "coarse_second")(
        along_z(rows), coarse_inverse, scalars
    )
    loads = after(loads, got)
    outs = call(
        final_kernel, [face] * 4, 18, "final", scratch=(whole,), grant=6
    )(
        masks, *gather_rows(loads), steps, z_deck, z_joint, y_deck, y_joint,
        image_deck, image_joint, res_deck, res_joint, corner_deck, corner_joint, w[0], w[2], *got,
    )
    return tuple(out[None, None] for out in outs)


def solution(mesh):
    mesh = Mesh(mesh.devices.reshape(Z, Y, X, 2), SPAN + DECK)
    block = P(SPAN, DECK, None, None)
    in_specs = (block, block, block, P(), block, block, P(SPAN, DECK, None))
    return jax.shard_map(
        local, mesh=mesh, in_specs=in_specs, out_specs=(block,) * 4, check_vma=False
    )
```

```python
import functools
import math

import jax
import jax.numpy as jnp
from jax import lax
from jax.experimental import pallas as pl
from jax.experimental.pallas import tpu as pltpu
from jax.sharding import Mesh
from jax.sharding import PartitionSpec as P

SPAN, DECK = ("z", "y"), ("x", "core")
SPANS, DECKS, Y, X, Z = 32, 8, 4, 4, 8
CASES, FACE, IFACE, NC, GB = 256, 256, 1024, 256, 4
WIDE = NC + 128
HALF = CASES // 2
PIECE = HALF // (Y * X)
SCALE = 1.0 / math.sqrt(SPANS * DECKS)
F32, BF16 = jnp.float32, jnp.bfloat16
VMEM = pl.BlockSpec(memory_space=pltpu.VMEM)
SMEM = pl.BlockSpec(memory_space=pltpu.SMEM)


def cyclic(block, axes, k):
    n = SPANS if axes == SPAN else DECKS
    return lax.ppermute(block, axes, [(i, (i + k) % n) for i in range(n)])


def near(block):
    return lax.ppermute(block, SPAN, [(i, i ^ 1) for i in range(SPANS)])


def far(block):
    return lax.ppermute(block, SPAN, [(i, (i + (1 if i % 2 else -1)) % SPANS) for i in range(SPANS)])


def swapped(block):
    return lax.ppermute(block, "core", [(0, 1), (1, 0)])


def parts(value):
    high = value.astype(BF16)
    return high, (value - high.astype(F32)).astype(BF16)


def product(left, right, dims=(((1,), (0,)), ((), ()))):
    dot = functools.partial(lax.dot_general, dimension_numbers=dims, preferred_element_type=F32)
    return dot(left[0], right[0]) + (dot(left[0], right[1]) + dot(left[1], right[0]))


TRANS = (((1,), (1,)), ((), ()))


def quarter(ref, i):
    return ref[:, i * FACE : (i + 1) * FACE]


def column(lane, *values):
    out = jnp.zeros((values[0].shape[0], 128), F32)
    for i, value in enumerate(values):
        out = jnp.where(lane == i, value, out)
    return out


def row_sum(value):
    return jnp.sum(value, axis=1, keepdims=True)


def cost(rows):
    return pl.CostEstimate(flops=6 * rows * IFACE * IFACE, bytes_accessed=8 << 20, transcendentals=0)


def call(body, outs, n_in, name, smem=(), scratch=(), estimate=None, grant=2):
    return pl.pallas_call(
        body,
        out_shape=tuple(s if isinstance(s, jax.ShapeDtypeStruct) else jax.ShapeDtypeStruct(s, F32) for s in outs),
        in_specs=[SMEM if i in smem else VMEM for i in range(n_in)],
        out_specs=tuple(VMEM for _ in outs),
        scratch_shapes=list(scratch),
        compiler_params=pltpu.CompilerParams(vmem_limit_bytes=grant << 20),
        cost_estimate=estimate,
        name=name,
    )


def keep(u_high, u_low, i, value):
    high, low = parts(value)
    u_high[:, i * FACE : (i + 1) * FACE] = high
    u_low[:, i * FACE : (i + 1) * FACE] = low


def position():
    span = lax.axis_index("z") * Y + lax.axis_index("y")
    return span, lax.axis_index("x") * 2 + lax.axis_index("core")


def live_row(ref, on):
    block = lax.broadcasted_iota(jnp.int32, (1, FACE), 1) // (FACE // GB)
    row = jnp.zeros((1, FACE), F32)
    for b in range(GB):
        row = jnp.where(block == b, ref[b].astype(F32), row)
    return row * on.astype(F32)


def faces_times(first, third, matrix, rows, i):
    at = slice(i * FACE, (i + 1) * FACE)
    return product(first, parts(matrix[rows : rows + FACE, at])) + product(
        third, parts(matrix[rows + 2 * FACE : rows + 3 * FACE, at])
    )


def by_span(near_value, far_value):
    odd = lax.rem(position()[0], 2) == 1
    return jnp.where(odd, far_value, near_value), jnp.where(odd, near_value, far_value)


def lives_kernel(active, out):
    out[...] = jnp.broadcast_to(live_row(active, position()[0] < SPANS - 1), (8, FACE))


def own_kernel(lives, deck, joint, matrix, part):
    first = parts((position()[1] < DECKS - 1).astype(F32) * deck[...])
    third = parts(lives[0:1, :] * joint[...])
    for i in range(4):
        part[:, i * FACE : (i + 1) * FACE] = faces_times(first, third, matrix, 0, i)


def behind_kernel(which, active, joint_behind, deck_behind, active_behind, part, matrix, *outs):
    span, across = position()
    ones = jnp.ones((1, FACE), F32)
    lives = (
        ones * (across < DECKS - 1).astype(F32),
        ones * (across > 0).astype(F32),
        live_row(active, span < SPANS - 1),
        live_row(active_behind, span > 0),
    )
    if len(outs) == 3:
        outs[2][...] = jnp.concatenate(lives + (jnp.zeros((4, FACE), F32),), axis=0)
    second, fourth = parts(lives[1] * deck_behind[...]), parts(lives[3] * joint_behind[...])
    values = [0.5 * (quarter(part, i) - faces_times(second, fourth, matrix, FACE, i)) for i in which]
    if which[0] == 2:
        values = by_span(*values)
    outs[0][...], outs[1][...] = values


def deck_jumps(masks, own, got, rows=slice(0, CASES)):
    return [masks[i : i + 1, :] * (own[i][rows, :] - got[i][rows, :]) for i in range(2)]


def span_jumps(masks, own, got, rows=slice(0, CASES)):
    ahead, behind = by_span(own[0][rows, :] - got[0][rows, :], own[1][rows, :] - got[1][rows, :])
    return [masks[2:3, :] * ahead, masks[3:4, :] * behind]


def two_quarters(jumps, matrix, corners, at):
    pair = parts(jnp.concatenate(jumps, axis=1))
    rows = slice(at, at + 2 * FACE)
    fields = [product(pair, parts(matrix[rows, i * FACE : (i + 1) * FACE])) for i in range(4)]
    return fields, product(pair, parts(corners[:, rows]), TRANS)


def flex_span_kernel(masks, f2, f3, g2, g3, matrix, corners, part, corner_part, third, fourth):
    third[...], fourth[...] = span_jumps(masks, (f2, f3), (g2, g3))
    fields, corner = two_quarters([third[...], fourth[...]], matrix, corners, 2 * FACE)
    for i in range(4):
        part[:, i * FACE : (i + 1) * FACE] = fields[i]
    corner_part[...] = corner


def flex_kernel(n_faces, masks, f0, f1, g0, g1, part, corner_part, third, fourth, matrix, corners, *refs):
    pairs, refs = refs[: 2 * n_faces], refs[2 * n_faces :]
    outs, (first, sent, held, table) = refs[:4], refs[4:]
    core = lax.axis_index("core")
    jumps = deck_jumps(masks, (f0, f1), (g0, g1))
    fields, corner = two_quarters(jumps, matrix, corners, 0)
    first[...] = jumps[0]
    jumps = jumps + [third[...], fourth[...]]
    total = jnp.zeros((CASES, 1), F32)
    values = [quarter(part, i) + fields[i] for i in range(4)]
    for i in range(4):
        total = total + row_sum(jumps[i] * values[i])
    if n_faces == 1:
        corner_quarters = [quarter(corners, i) for i in range(4)]
        corner_quarters[2:] = by_span(*corner_quarters[2:])
        values[2:] = by_span(*values[2:])
        for i in range(4):
            outs[i][: CASES, :] = values[i]
            outs[i][CASES:, :] = corner_quarters[i]
    else:
        for i in range(4):
            outs[i][...] = values[i]
    sums = [
        row_sum(masks[0:1, :] * pairs[2 * k][...] * first[...] + masks[2:3, :] * pairs[2 * k + 1][...] * third[...])
        for k in range(n_faces)
    ]
    table[:, :NC] = corner_part[...] + corner
    lane = lax.broadcasted_iota(jnp.int32, (CASES, 128), 1)
    table[:, NC:] = column(lane, total, *sums)
    held[...] = table[pl.ds(pl.multiple_of(core * HALF, HALF), HALF), :]
    sent[...] = table[pl.ds(pl.multiple_of((1 - core) * HALF, HALF), HALF), :]


def total_of(got):
    part = got[0]
    for k in range(1, Z):
        part = part + got[k]
    return part


def first_coarse_kernel(got, coarse, out, scalars):
    part = total_of(got)
    total = part[:, :NC]
    load = SCALE * product(parts(total), parts(coarse[...]))
    curv = part[:, NC : NC + 1] + row_sum(load * total)
    rz = part[:, NC + 1 : NC + 2]
    lane = lax.broadcasted_iota(jnp.int32, (PIECE, 128), 1)
    row = jnp.concatenate([load, column(lane, rz / curv)], axis=1)
    for k in range(Y * X):
        out[k] = row
    scalars[...] = column(lane, rz, curv)


def second_coarse_kernel(got, coarse, scalars, out):
    part = total_of(got)
    total = part[:, :NC]
    load = SCALE * product(parts(total), parts(coarse[...]))
    own = part[:, NC : NC + 1] + row_sum(load * total)
    new = part[:, NC + 1 : NC + 2]
    cross = part[:, NC + 2 : NC + 3]
    rz, curv = scalars[:, 0:1], scalars[:, 1:2]
    ratio = new / rz
    second = new / (own + ratio * (2.0 * cross + ratio * curv))
    lane = lax.broadcasted_iota(jnp.int32, (PIECE, 128), 1)
    row = jnp.concatenate([second * load, column(lane, second, second * ratio)], axis=1)
    for k in range(Y * X):
        out[k] = row


def place_rows(mine, other, whole):
    core = lax.axis_index("core")
    whole[pl.ds(pl.multiple_of(core * HALF, HALF), HALF), :] = mine[...]
    whole[pl.ds(pl.multiple_of((1 - core) * HALF, HALF), HALF), :] = other[...]


def precond_kernel(masks, mine, other, f0, f1, f2, f3, g0, g1, g2, g3,
                   deck, joint, deck_behind, joint_behind, matrix,
                   v2, v3, u_high, u_low, image_deck, image_joint, res_deck, res_joint,
                   corner_deck, corner_joint, steps, whole):
    place_rows(mine, other, whole)
    load = parts(whole[:, :NC])
    step = whole[:, NC : NC + 1]
    steps[...] = whole[:, NC:]
    gaps = (deck, deck_behind, joint, joint_behind)
    low = slice(CASES, 2 * CASES)
    images = deck_jumps(masks, (f0, f1), (g0, g1)) + span_jumps(masks, (f2, f3), (g2, g3))
    corner = deck_jumps(masks, (f0, f1), (g0, g1), low) + span_jumps(masks, (f2, f3), (g2, g3), low)
    for i in range(4):
        image = images[i] + product(load, parts(corner[i]))
        gap = masks[i : i + 1, :] * gaps[i][...]
        res = (gap if i % 2 == 0 else -gap) - step * image
        if i == 0:
            corner_deck[...], image_deck[...], res_deck[...] = corner[i], image, res
        if i == 2:
            corner_joint[...], image_joint[...], res_joint[...] = corner[i], image, res
        keep(u_high, u_low, i, res)

    span_quarters(u_high, u_low, matrix, v2, v3)


def two_of(first, u_high, u_low, matrix):
    pair = u_high[...], u_low[...]
    return [0.5 * product(pair, parts(quarter(matrix, first + i))) for i in range(2)]


def span_quarters(u_high, u_low, matrix, v2, v3):
    v2[...], v3[...] = by_span(*two_of(2, u_high, u_low, matrix))


def deck_quarters(u_high, u_low, matrix, v0, v1):
    v0[...], v1[...] = two_of(0, u_high, u_low, matrix)


def final_kernel(masks, mine, other, steps, z_deck, z_joint, y_deck, y_joint,
                 image_deck, image_joint, res_deck, res_joint, corner_deck, corner_joint,
                 f0, f2, g0, g2, sol_deck, sol_joint, out_deck, out_joint, whole):
    place_rows(mine, other, whole)
    load = parts(whole[:, :NC])
    second, mixed = whole[:, NC : NC + 1], whole[:, NC + 1 : NC + 2]
    first = steps[:, 0:1] + mixed
    sol_deck[...] = first * z_deck[...] + second * y_deck[...]
    sol_joint[...] = first * z_joint[...] + second * y_joint[...]
    for i, res, field, ahead, image, corner, out in (
        (0, res_deck, f0, g0, image_deck, corner_deck, out_deck),
        (2, res_joint, f2, g2, image_joint, corner_joint, out_joint),
    ):
        reaction = masks[i : i + 1, :] * (field[...] - ahead[...])
        out[...] = (
            res[...] - second * reaction - mixed * image[...] - product(load, parts(corner[...]))
        )


def exchange(field):
    right, left, to_near, to_far = field
    right_got, left_got = cyclic(right, DECK, 1), cyclic(left, DECK, -1)
    return left_got, right_got, near(to_near), far(to_far)


def add_kernel(held, got, out):
    for k in range(Y * X):
        at = slice(k * PIECE, (k + 1) * PIECE)
        out[k] = held[at, :] + got[at, :]


def spread_kernel(got, out):
    part = got[0]
    for k in range(1, Y * X):
        part = part + got[k]
    for k in range(Z):
        out[k] = part


def scatter_rows(sent, held):
    (block,) = call(add_kernel, [(Y * X, PIECE, WIDE)], 2, "add")(held, swapped(sent))
    return lax.all_to_all(block, ("y", "x"), 0, 0)


def along_z(got):
    (copies,) = call(spread_kernel, [(Z, PIECE, WIDE)], 1, "spread")(got)
    return lax.all_to_all(copies, "z", 0, 0)


def gather_rows(copies):
    mine = lax.all_to_all(copies, ("y", "x"), 0, 0).reshape(HALF, WIDE)
    return mine, swapped(mine)


def after(values, *others):
    return lax.optimization_barrier((values, others))[0]


def local(flex, precond, corner_map, coarse_inverse, gap_deck, gap_joint, active):
    flex, precond, corners = flex[0, 0], precond[0, 0], corner_map[0, 0]
    deck, joint, active = gap_deck[0, 0], gap_joint[0, 0], active[0, 0]
    face, pair, field, stacked = (CASES, FACE), [(CASES, FACE)] * 2, [(CASES, FACE)] * 4, [(2 * CASES, FACE)] * 4
    wide, half, copies = (CASES, IFACE), (HALF, WIDE), (Y * X, PIECE, WIDE)
    narrow = [jax.ShapeDtypeStruct(wide, BF16)] * 2
    whole = pltpu.VMEM((CASES, WIDE), F32)

    def flexed(n_faces, v, name, shapes, *pairs):
        got = exchange(v)
        part, corner, third, fourth = call(
            flex_span_kernel, [wide, (CASES, NC), face, face], 7, name + "_span",
            estimate=cost(CASES // 2), grant=10,
        )(masks, *v[2:], *got[2:], flex, corners)
        *w, first, sent, held = call(
            functools.partial(flex_kernel, n_faces), shapes + [face, half, half], 11 + 2 * n_faces,
            name, scratch=(whole,), estimate=cost(CASES // 2), grant=10,
        )(masks, *v[:2], *got[:2], part, corner, third, fourth, flex, corners, *pairs)
        return *w, first, third, sent, held

    joint_behind = cyclic(joint, SPAN, 1)
    deck_behind = cyclic(deck, DECK, 1)
    active_behind = cyclic(active, SPAN, 1)
    gaps = (deck, joint, deck_behind, joint_behind)
    (lives,) = call(lives_kernel, [(8, FACE)], 1, "lives", smem=(0,), estimate=cost(4 * CASES))(active)
    (part,) = call(
        own_kernel, [wide], 4, "own", estimate=cost(CASES // 2), grant=10
    )(lives, deck, joint, precond)
    behind = (active, joint_behind, deck_behind, active_behind, part, precond)
    v2, v3, masks = call(
        functools.partial(behind_kernel, (2, 3)), pair + [(8, FACE)], 6, "behind_span",
        smem=(0, 3), estimate=cost(CASES // 4), grant=10,
    )(*behind)
    v0, v1 = call(
        functools.partial(behind_kernel, (0, 1)), pair, 6, "behind_deck",
        smem=(0, 3), estimate=cost(CASES // 4), grant=10,
    )(*behind)
    *w, z_deck, z_joint, sent, held = flexed(1, (v0, v1, v2, v3), "flex_first", stacked, deck, joint)
    rows = scatter_rows(sent, held)
    loads, scalars = call(first_coarse_kernel, [copies, (PIECE, 128)], 2, "coarse_first")(
        along_z(rows), coarse_inverse
    )
    got = exchange(after(w, loads))
    v2, v3, *u, image_deck, image_joint, res_deck, res_joint, corner_deck, corner_joint, steps = call(
        precond_kernel, pair + narrow + [face] * 6 + [(CASES, 128)], 16, "precond_span",
        scratch=(whole,), estimate=cost(CASES // 2), grant=10,
    )(masks, *gather_rows(loads), *w, *got, *gaps, precond)
    v0, v1 = call(
        deck_quarters, pair, 3, "precond_deck", estimate=cost(CASES // 2), grant=10
    )(*u, precond)
    *w, y_deck, y_joint, sent, held = flexed(
        2, (v0, v1, v2, v3), "flex_second", field, res_deck, res_joint, image_deck, image_joint
    )
    rows = scatter_rows(sent, held)
    left, behind = after((w[1], w[3]), rows)
    got = cyclic(left, DECK, -1), cyclic(behind, SPAN, -1)
    (loads,) = call(second_coarse_kernel, [copies], 3, "coarse_second")(
        along_z(rows), coarse_inverse, scalars
    )
    loads = after(loads, got)
    outs = call(
        final_kernel, [face] * 4, 18, "final", scratch=(whole,), grant=6
    )(
        masks, *gather_rows(loads), steps, z_deck, z_joint, y_deck, y_joint,
        image_deck, image_joint, res_deck, res_joint, corner_deck, corner_joint, w[0], w[2], *got,
    )
    return tuple(out[None, None] for out in outs)


def solution(mesh):
    mesh = Mesh(mesh.devices.reshape(Z, Y, X, 2), SPAN + DECK)
    block = P(SPAN, DECK, None, None)
    in_specs = (block, block, block, P(), block, block, P(SPAN, DECK, None))
    return jax.shard_map(
        local, mesh=mesh, in_specs=in_specs, out_specs=(block,) * 4, check_vma=False
    )
```

```python
import functools
import math

import jax
import jax.numpy as jnp
from jax import lax
from jax.experimental import pallas as pl
from jax.experimental.pallas import tpu as pltpu
from jax.sharding import Mesh
from jax.sharding import PartitionSpec as P

SPAN, DECK = ("z", "y"), ("x", "core")
SPANS, DECKS, Y, X, Z = 32, 8, 4, 4, 8
CASES, FACE, IFACE, NC, GB = 256, 256, 1024, 256, 4
WIDE = NC + 128
HALF = CASES // 2
PIECE = HALF // (Y * X)
SCALE = 1.0 / math.sqrt(SPANS * DECKS)
F32, BF16 = jnp.float32, jnp.bfloat16
VMEM = pl.BlockSpec(memory_space=pltpu.VMEM)
SMEM = pl.BlockSpec(memory_space=pltpu.SMEM)


def cyclic(block, axes, k):
    n = SPANS if axes == SPAN else DECKS
    return lax.ppermute(block, axes, [(i, (i + k) % n) for i in range(n)])


def near(block):
    return lax.ppermute(block, SPAN, [(i, i ^ 1) for i in range(SPANS)])


def far(block):
    return lax.ppermute(block, SPAN, [(i, (i + (1 if i % 2 else -1)) % SPANS) for i in range(SPANS)])


def swapped(block):
    return lax.ppermute(block, "core", [(0, 1), (1, 0)])


def parts(value):
    high = value.astype(BF16)
    return high, (value - high.astype(F32)).astype(BF16)


def product(left, right, dims=(((1,), (0,)), ((), ()))):
    dot = functools.partial(lax.dot_general, dimension_numbers=dims, preferred_element_type=F32)
    return dot(left[0], right[0]) + (dot(left[0], right[1]) + dot(left[1], right[0]))


TRANS = (((1,), (1,)), ((), ()))


def quarter(ref, i):
    return ref[:, i * FACE : (i + 1) * FACE]


def column(lane, *values):
    out = jnp.zeros((values[0].shape[0], 128), F32)
    for i, value in enumerate(values):
        out = jnp.where(lane == i, value, out)
    return out


def row_sum(value):
    return jnp.sum(value, axis=1, keepdims=True)


def cost(rows):
    return pl.CostEstimate(flops=6 * rows * IFACE * IFACE, bytes_accessed=8 << 20, transcendentals=0)


def call(body, outs, n_in, name, smem=(), scratch=(), estimate=None, grant=2):
    return pl.pallas_call(
        body,
        out_shape=tuple(s if isinstance(s, jax.ShapeDtypeStruct) else jax.ShapeDtypeStruct(s, F32) for s in outs),
        in_specs=[SMEM if i in smem else VMEM for i in range(n_in)],
        out_specs=tuple(VMEM for _ in outs),
        scratch_shapes=list(scratch),
        compiler_params=pltpu.CompilerParams(vmem_limit_bytes=grant << 20),
        cost_estimate=estimate,
        name=name,
    )


def keep(u_high, u_low, i, value):
    high, low = parts(value)
    u_high[:, i * FACE : (i + 1) * FACE] = high
    u_low[:, i * FACE : (i + 1) * FACE] = low


def position():
    span = lax.axis_index("z") * Y + lax.axis_index("y")
    return span, lax.axis_index("x") * 2 + lax.axis_index("core")


def live_row(ref, on):
    block = lax.broadcasted_iota(jnp.int32, (1, FACE), 1) // (FACE // GB)
    row = jnp.zeros((1, FACE), F32)
    for b in range(GB):
        row = jnp.where(block == b, ref[b].astype(F32), row)
    return row * on.astype(F32)


def block_of(pair, rows, columns):
    return pair[0][rows, columns], pair[1][rows, columns]


def faces_times(first, third, matrix, row, i):
    at = slice(i * FACE, (i + 1) * FACE)
    return product(first, block_of(matrix, slice(row, row + FACE), at)) + product(
        third, block_of(matrix, slice(row + 2 * FACE, row + 3 * FACE), at)
    )


def split_kernel(matrix, high, low):
    for i in range(4):
        keep(high, low, i, quarter(matrix, i))


def fourth_kernel(joint_behind, lives_behind, high, low):
    high[...], low[...] = parts(lives_behind[0:1, :] * joint_behind[...])


def by_span(near_value, far_value):
    odd = lax.rem(position()[0], 2) == 1
    return jnp.where(odd, far_value, near_value), jnp.where(odd, near_value, far_value)


def lives_kernel(active, out):
    out[...] = jnp.broadcast_to(live_row(active, position()[0] < SPANS - 1), (8, FACE))


def own_kernel(lives, deck, joint, high, low, part):
    first = parts((position()[1] < DECKS - 1).astype(F32) * deck[...])
    third = parts(lives[0:1, :] * joint[...])
    for i in range(4):
        part[:, i * FACE : (i + 1) * FACE] = faces_times(first, third, (high, low), 0, i)


def behind_kernel(which, joint_high, joint_low, deck_behind, lives, lives_behind, part, high, low, *outs):
    _, across = position()
    ones = jnp.ones((1, FACE), F32)
    lives = (
        ones * (across < DECKS - 1).astype(F32),
        ones * (across > 0).astype(F32),
        lives[0:1, :],
        lives_behind[0:1, :],
    )
    if len(outs) == 3:
        outs[2][...] = jnp.concatenate(lives + (jnp.zeros((4, FACE), F32),), axis=0)
    second, fourth = parts(lives[1] * deck_behind[...]), (joint_high[...], joint_low[...])
    values = [0.5 * (quarter(part, i) - faces_times(second, fourth, (high, low), FACE, i)) for i in which]
    if which[0] == 2:
        values = by_span(*values)
    outs[0][...], outs[1][...] = values


def deck_jumps(masks, own, got, rows=slice(0, CASES)):
    return [masks[i : i + 1, :] * (own[i][rows, :] - got[i][rows, :]) for i in range(2)]


def span_jumps(masks, own, got, rows=slice(0, CASES)):
    ahead, behind = by_span(own[0][rows, :] - got[0][rows, :], own[1][rows, :] - got[1][rows, :])
    return [masks[2:3, :] * ahead, masks[3:4, :] * behind]


def two_quarters(jumps, matrix, corners, at):
    pair = parts(jnp.concatenate(jumps, axis=1))
    rows = slice(at, at + 2 * FACE)
    fields = [product(pair, block_of(matrix, rows, slice(i * FACE, (i + 1) * FACE))) for i in range(4)]
    return fields, product(pair, parts(corners[:, rows]), TRANS)


def flex_span_kernel(masks, f2, f3, g2, g3, high, low, corners, part, corner_part, third, fourth):
    third[...], fourth[...] = span_jumps(masks, (f2, f3), (g2, g3))
    fields, corner = two_quarters([third[...], fourth[...]], (high, low), corners, 2 * FACE)
    for i in range(4):
        part[:, i * FACE : (i + 1) * FACE] = fields[i]
    corner_part[...] = corner


def flex_kernel(n_faces, masks, f0, f1, g0, g1, part, corner_part, third, fourth, high, low, corners, *refs):
    pairs, refs = refs[: 2 * n_faces], refs[2 * n_faces :]
    outs, (first, sent, held, table) = refs[:4], refs[4:]
    core = lax.axis_index("core")
    jumps = deck_jumps(masks, (f0, f1), (g0, g1))
    fields, corner = two_quarters(jumps, (high, low), corners, 0)
    first[...] = jumps[0]
    jumps = jumps + [third[...], fourth[...]]
    total = jnp.zeros((CASES, 1), F32)
    values = [quarter(part, i) + fields[i] for i in range(4)]
    for i in range(4):
        total = total + row_sum(jumps[i] * values[i])
    if n_faces == 1:
        corner_quarters = [quarter(corners, i) for i in range(4)]
        corner_quarters[2:] = by_span(*corner_quarters[2:])
        values[2:] = by_span(*values[2:])
        for i in range(4):
            outs[i][: CASES, :] = values[i]
            outs[i][CASES:, :] = corner_quarters[i]
    else:
        for i in range(4):
            outs[i][...] = values[i]
    sums = [
        row_sum(masks[0:1, :] * pairs[2 * k][...] * first[...] + masks[2:3, :] * pairs[2 * k + 1][...] * third[...])
        for k in range(n_faces)
    ]
    table[:, :NC] = corner_part[...] + corner
    lane = lax.broadcasted_iota(jnp.int32, (CASES, 128), 1)
    table[:, NC:] = column(lane, total, *sums)
    held[...] = table[pl.ds(pl.multiple_of(core * HALF, HALF), HALF), :]
    sent[...] = table[pl.ds(pl.multiple_of((1 - core) * HALF, HALF), HALF), :]


def total_of(got):
    part = got[0]
    for k in range(1, Z):
        part = part + got[k]
    return part


def first_coarse_kernel(got, coarse, out, scalars):
    part = total_of(got)
    total = part[:, :NC]
    load = SCALE * product(parts(total), parts(coarse[...]))
    curv = part[:, NC : NC + 1] + row_sum(load * total)
    rz = part[:, NC + 1 : NC + 2]
    lane = lax.broadcasted_iota(jnp.int32, (PIECE, 128), 1)
    row = jnp.concatenate([load, column(lane, rz / curv)], axis=1)
    for k in range(Y * X):
        out[k] = row
    scalars[...] = column(lane, rz, curv)


def second_coarse_kernel(got, coarse, scalars, out):
    part = total_of(got)
    total = part[:, :NC]
    load = SCALE * product(parts(total), parts(coarse[...]))
    own = part[:, NC : NC + 1] + row_sum(load * total)
    new = part[:, NC + 1 : NC + 2]
    cross = part[:, NC + 2 : NC + 3]
    rz, curv = scalars[:, 0:1], scalars[:, 1:2]
    ratio = new / rz
    second = new / (own + ratio * (2.0 * cross + ratio * curv))
    lane = lax.broadcasted_iota(jnp.int32, (PIECE, 128), 1)
    row = jnp.concatenate([second * load, column(lane, second, second * ratio)], axis=1)
    for k in range(Y * X):
        out[k] = row


def place_rows(mine, other, whole):
    core = lax.axis_index("core")
    whole[pl.ds(pl.multiple_of(core * HALF, HALF), HALF), :] = mine[...]
    whole[pl.ds(pl.multiple_of((1 - core) * HALF, HALF), HALF), :] = other[...]


def precond_kernel(masks, mine, other, f0, f1, f2, f3, g0, g1, g2, g3,
                   deck, joint, deck_behind, joint_behind, high, low,
                   v2, v3, u_high, u_low, image_deck, image_joint, res_deck, res_joint,
                   corner_deck, corner_joint, steps, whole):
    place_rows(mine, other, whole)
    load = parts(whole[:, :NC])
    step = whole[:, NC : NC + 1]
    steps[...] = whole[:, NC:]
    gaps = (deck, deck_behind, joint, joint_behind)
    under = slice(CASES, 2 * CASES)
    images = deck_jumps(masks, (f0, f1), (g0, g1)) + span_jumps(masks, (f2, f3), (g2, g3))
    corner = deck_jumps(masks, (f0, f1), (g0, g1), under) + span_jumps(masks, (f2, f3), (g2, g3), under)
    for i in range(4):
        image = images[i] + product(load, parts(corner[i]))
        gap = masks[i : i + 1, :] * gaps[i][...]
        res = (gap if i % 2 == 0 else -gap) - step * image
        if i == 0:
            corner_deck[...], image_deck[...], res_deck[...] = corner[i], image, res
        if i == 2:
            corner_joint[...], image_joint[...], res_joint[...] = corner[i], image, res
        keep(u_high, u_low, i, res)

    span_quarters(u_high, u_low, high, low, v2, v3)


def two_of(first, u_high, u_low, high, low):
    pair, rows = (u_high[...], u_low[...]), slice(0, IFACE)
    return [
        0.5 * product(pair, block_of((high, low), rows, slice(i * FACE, (i + 1) * FACE)))
        for i in (first, first + 1)
    ]


def span_quarters(u_high, u_low, high, low, v2, v3):
    v2[...], v3[...] = by_span(*two_of(2, u_high, u_low, high, low))


def deck_quarters(u_high, u_low, high, low, v0, v1):
    v0[...], v1[...] = two_of(0, u_high, u_low, high, low)


def final_kernel(masks, mine, other, steps, z_deck, z_joint, y_deck, y_joint,
                 image_deck, image_joint, res_deck, res_joint, corner_deck, corner_joint,
                 f0, f2, g0, g2, sol_deck, sol_joint, out_deck, out_joint, whole):
    place_rows(mine, other, whole)
    load = parts(whole[:, :NC])
    second, mixed = whole[:, NC : NC + 1], whole[:, NC + 1 : NC + 2]
    first = steps[:, 0:1] + mixed
    sol_deck[...] = first * z_deck[...] + second * y_deck[...]
    sol_joint[...] = first * z_joint[...] + second * y_joint[...]
    for i, res, field, ahead, image, corner, out in (
        (0, res_deck, f0, g0, image_deck, corner_deck, out_deck),
        (2, res_joint, f2, g2, image_joint, corner_joint, out_joint),
    ):
        reaction = masks[i : i + 1, :] * (field[...] - ahead[...])
        out[...] = (
            res[...] - second * reaction - mixed * image[...] - product(load, parts(corner[...]))
        )


def exchange(field):
    right, left, to_near, to_far = field
    right_got, left_got = cyclic(right, DECK, 1), cyclic(left, DECK, -1)
    return left_got, right_got, near(to_near), far(to_far)


def add_kernel(held, got, out):
    for k in range(Y * X):
        at = slice(k * PIECE, (k + 1) * PIECE)
        out[k] = held[at, :] + got[at, :]


def spread_kernel(got, out):
    part = got[0]
    for k in range(1, Y * X):
        part = part + got[k]
    for k in range(Z):
        out[k] = part


def scatter_rows(sent, held):
    (block,) = call(add_kernel, [(Y * X, PIECE, WIDE)], 2, "add")(held, swapped(sent))
    return lax.all_to_all(block, ("y", "x"), 0, 0)


def along_z(got):
    (copies,) = call(spread_kernel, [(Z, PIECE, WIDE)], 1, "spread")(got)
    return lax.all_to_all(copies, "z", 0, 0)


def gather_rows(copies):
    mine = lax.all_to_all(copies, ("y", "x"), 0, 0).reshape(HALF, WIDE)
    return mine, swapped(mine)


def after(values, *others):
    return lax.optimization_barrier((values, others))[0]


def local(flex, precond, corner_map, coarse_inverse, gap_deck, gap_joint, active):
    flex, precond, corners = flex[0, 0], precond[0, 0], corner_map[0, 0]
    deck, joint, active = gap_deck[0, 0], gap_joint[0, 0], active[0, 0]
    face, pair, field, stacked = (CASES, FACE), [(CASES, FACE)] * 2, [(CASES, FACE)] * 4, [(2 * CASES, FACE)] * 4
    wide, half, copies = (CASES, IFACE), (HALF, WIDE), (Y * X, PIECE, WIDE)
    narrow = [jax.ShapeDtypeStruct(wide, BF16)] * 2
    whole = pltpu.VMEM((CASES, WIDE), F32)

    def flexed(n_faces, v, name, shapes, *pairs):
        got = exchange(v)
        part, corner, third, fourth = call(
            flex_span_kernel, [wide, (CASES, NC), face, face], 8, name + "_span",
            estimate=cost(CASES // 2), grant=10,
        )(masks, *v[2:], *got[2:], *flex_pair, corners)
        *w, first, sent, held = call(
            functools.partial(flex_kernel, n_faces), shapes + [face, half, half], 12 + 2 * n_faces,
            name, scratch=(whole,), estimate=cost(CASES // 2), grant=10,
        )(masks, *v[:2], *got[:2], part, corner, third, fourth, *flex_pair, corners, *pairs)
        return *w, first, third, sent, held

    joint_behind = cyclic(joint, SPAN, 1)
    (lives,) = call(lives_kernel, [(8, FACE)], 1, "lives", smem=(0,), estimate=cost(4 * CASES))(active)
    deck_behind = cyclic(after(deck, lives), DECK, 1)
    lives_behind = cyclic(lives, SPAN, 1)
    gaps = (deck, joint, deck_behind, joint_behind)
    halves = [jax.ShapeDtypeStruct((IFACE, IFACE), BF16)] * 2
    pre_pair, flex_pair = (
        call(split_kernel, halves, 1, name, estimate=cost(CASES // 4), grant=4)(matrix)
        for matrix, name in ((precond, "split_precond"), (flex, "split_flex"))
    )
    (part,) = call(
        own_kernel, [wide], 5, "own", estimate=cost(CASES // 2), grant=10
    )(lives, deck, joint, *pre_pair)
    fourth = call(
        fourth_kernel, [jax.ShapeDtypeStruct(face, BF16)] * 2, 2, "fourth", estimate=cost(CASES // 8)
    )(joint_behind, lives_behind)
    behind = (*fourth, deck_behind, lives, lives_behind, part, *pre_pair)
    v2, v3, masks = call(
        functools.partial(behind_kernel, (2, 3)), pair + [(8, FACE)], 8, "behind_span",
        estimate=cost(CASES // 4), grant=10,
    )(*behind)
    v0, v1 = call(
        functools.partial(behind_kernel, (0, 1)), pair, 8, "behind_deck",
        estimate=cost(CASES // 4), grant=10,
    )(*behind)
    *w, z_deck, z_joint, sent, held = flexed(1, (v0, v1, v2, v3), "flex_first", stacked, deck, joint)
    rows = scatter_rows(sent, held)
    loads, scalars = call(first_coarse_kernel, [copies, (PIECE, 128)], 2, "coarse_first")(
        along_z(rows), coarse_inverse
    )
    *early, _ = after(w, rows)
    got = exchange((*early, after(w[3], loads)))
    loads = after(loads, got[:3])
    v2, v3, *u, image_deck, image_joint, res_deck, res_joint, corner_deck, corner_joint, steps = call(
        precond_kernel, pair + narrow + [face] * 6 + [(CASES, 128)], 17, "precond_span",
        scratch=(whole,), estimate=cost(CASES // 2), grant=10,
    )(masks, *gather_rows(loads), *w, *got, *gaps, *pre_pair)
    v0, v1 = call(
        deck_quarters, pair, 4, "precond_deck", estimate=cost(CASES // 2), grant=10
    )(*u, *pre_pair)
    *w, y_deck, y_joint, sent, held = flexed(
        2, (v0, v1, v2, v3), "flex_second", field, res_deck, res_joint, image_deck, image_joint
    )
    rows = scatter_rows(sent, held)
    left, behind = after((w[1], w[3]), rows)
    got = cyclic(left, DECK, -1), cyclic(behind, SPAN, -1)
    (loads,) = call(second_coarse_kernel, [copies], 3, "coarse_second")(
        along_z(rows), coarse_inverse, scalars
    )
    loads = after(loads, got)
    outs = call(
        final_kernel, [face] * 4, 18, "final", scratch=(whole,), grant=6
    )(
        masks, *gather_rows(loads), steps, z_deck, z_joint, y_deck, y_joint,
        image_deck, image_joint, res_deck, res_joint, corner_deck, corner_joint, w[0], w[2], *got,
    )
    return tuple(out[None, None] for out in outs)


def solution(mesh):
    mesh = Mesh(mesh.devices.reshape(Z, Y, X, 2), SPAN + DECK)
    block = P(SPAN, DECK, None, None)
    in_specs = (block, block, block, P(), block, block, P(SPAN, DECK, None))
    return jax.shard_map(
        local, mesh=mesh, in_specs=in_specs, out_specs=(block,) * 4, check_vma=False
    )
```

```python
import functools
import math

import jax
import jax.numpy as jnp
from jax import lax
from jax.experimental import pallas as pl
from jax.experimental.pallas import tpu as pltpu
from jax.sharding import Mesh
from jax.sharding import PartitionSpec as P

SPAN, DECK = ("z", "y"), ("x", "core")
SPANS, DECKS, Y, X, Z = 32, 8, 4, 4, 8
CASES, FACE, IFACE, NC, GB = 256, 256, 1024, 256, 4
WIDE = NC + 128
HALF = CASES // 2
PIECE = HALF // (Y * X)
SCALE = 1.0 / math.sqrt(SPANS * DECKS)
F32, BF16 = jnp.float32, jnp.bfloat16
VMEM = pl.BlockSpec(memory_space=pltpu.VMEM)
SMEM = pl.BlockSpec(memory_space=pltpu.SMEM)


def cyclic(block, axes, k):
    n = SPANS if axes == SPAN else DECKS
    return lax.ppermute(block, axes, [(i, (i + k) % n) for i in range(n)])


def near(block):
    return lax.ppermute(block, SPAN, [(i, i ^ 1) for i in range(SPANS)])


def far(block):
    return lax.ppermute(block, SPAN, [(i, (i + (1 if i % 2 else -1)) % SPANS) for i in range(SPANS)])


def swapped(block):
    return lax.ppermute(block, "core", [(0, 1), (1, 0)])


def parts(value):
    high = value.astype(BF16)
    return high, (value - high.astype(F32)).astype(BF16)


def product(left, right, dims=(((1,), (0,)), ((), ()))):
    dot = functools.partial(lax.dot_general, dimension_numbers=dims, preferred_element_type=F32)
    return dot(left[0], right[0]) + (dot(left[0], right[1]) + dot(left[1], right[0]))


TRANS = (((1,), (1,)), ((), ()))


def quarter(ref, i):
    return ref[:, i * FACE : (i + 1) * FACE]


def column(lane, *values):
    out = jnp.zeros((values[0].shape[0], 128), F32)
    for i, value in enumerate(values):
        out = jnp.where(lane == i, value, out)
    return out


def row_sum(value):
    return jnp.sum(value, axis=1, keepdims=True)


def cost(rows):
    return pl.CostEstimate(flops=6 * rows * IFACE * IFACE, bytes_accessed=8 << 20, transcendentals=0)


def call(body, outs, n_in, name, smem=(), scratch=(), estimate=None, grant=2):
    return pl.pallas_call(
        body,
        out_shape=tuple(s if isinstance(s, jax.ShapeDtypeStruct) else jax.ShapeDtypeStruct(s, F32) for s in outs),
        in_specs=[SMEM if i in smem else VMEM for i in range(n_in)],
        out_specs=tuple(VMEM for _ in outs),
        scratch_shapes=list(scratch),
        compiler_params=pltpu.CompilerParams(vmem_limit_bytes=grant << 20),
        cost_estimate=estimate,
        name=name,
    )


def keep(u_high, u_low, i, value):
    high, low = parts(value)
    u_high[:, i * FACE : (i + 1) * FACE] = high
    u_low[:, i * FACE : (i + 1) * FACE] = low


def position():
    span = lax.axis_index("z") * Y + lax.axis_index("y")
    return span, lax.axis_index("x") * 2 + lax.axis_index("core")


def live_row(ref, on):
    block = lax.broadcasted_iota(jnp.int32, (1, FACE), 1) // (FACE // GB)
    row = jnp.zeros((1, FACE), F32)
    for b in range(GB):
        row = jnp.where(block == b, ref[b].astype(F32), row)
    return row * on.astype(F32)


def block_of(pair, rows, columns):
    return pair[0][rows, columns], pair[1][rows, columns]


def faces_times(first, third, matrix, row, i):
    at = slice(i * FACE, (i + 1) * FACE)
    return product(first, block_of(matrix, slice(row, row + FACE), at)) + product(
        third, block_of(matrix, slice(row + 2 * FACE, row + 3 * FACE), at)
    )


def split_kernel(matrix, high, low):
    for i in range(4):
        keep(high, low, i, quarter(matrix, i))


def fourth_kernel(joint_behind, lives_behind, high, low):
    high[...], low[...] = parts(lives_behind[0:1, :] * joint_behind[...])


def by_span(near_value, far_value):
    odd = lax.rem(position()[0], 2) == 1
    return jnp.where(odd, far_value, near_value), jnp.where(odd, near_value, far_value)


def lives_kernel(active, out):
    out[...] = jnp.broadcast_to(live_row(active, position()[0] < SPANS - 1), (8, FACE))


def own_kernel(lives, deck, joint, high, low, part):
    first = parts((position()[1] < DECKS - 1).astype(F32) * deck[...])
    third = parts(lives[0:1, :] * joint[...])
    for i in range(4):
        part[:, i * FACE : (i + 1) * FACE] = faces_times(first, third, (high, low), 0, i)


def behind_kernel(which, joint_high, joint_low, deck_behind, lives, lives_behind, part, high, low, *outs):
    _, across = position()
    ones = jnp.ones((1, FACE), F32)
    lives = (
        ones * (across < DECKS - 1).astype(F32),
        ones * (across > 0).astype(F32),
        lives[0:1, :],
        lives_behind[0:1, :],
    )
    if len(outs) == 3:
        outs[2][...] = jnp.concatenate(lives + (jnp.zeros((4, FACE), F32),), axis=0)
    second, fourth = parts(lives[1] * deck_behind[...]), (joint_high[...], joint_low[...])
    values = [0.5 * (quarter(part, i) - faces_times(second, fourth, (high, low), FACE, i)) for i in which]
    if which[0] == 2:
        values = by_span(*values)
    outs[0][...], outs[1][...] = values


def deck_jumps(masks, own, got, rows=slice(0, CASES)):
    return [masks[i : i + 1, :] * (own[i][rows, :] - got[i][rows, :]) for i in range(2)]


def span_jumps(masks, own, got, rows=slice(0, CASES)):
    ahead, behind = by_span(own[0][rows, :] - got[0][rows, :], own[1][rows, :] - got[1][rows, :])
    return [masks[2:3, :] * ahead, masks[3:4, :] * behind]


def two_quarters(jumps, matrix, corners, at):
    pair = parts(jnp.concatenate(jumps, axis=1))
    rows = slice(at, at + 2 * FACE)
    fields = [product(pair, block_of(matrix, rows, slice(i * FACE, (i + 1) * FACE))) for i in range(4)]
    return fields, product(pair, parts(corners[:, rows]), TRANS)


def flex_span_kernel(masks, f2, f3, g2, g3, high, low, corners, part, corner_part, third, fourth):
    third[...], fourth[...] = span_jumps(masks, (f2, f3), (g2, g3))
    fields, corner = two_quarters([third[...], fourth[...]], (high, low), corners, 2 * FACE)
    for i in range(4):
        part[:, i * FACE : (i + 1) * FACE] = fields[i]
    corner_part[...] = corner


def flex_kernel(n_faces, masks, f0, f1, g0, g1, part, corner_part, third, fourth, high, low, corners, *refs):
    pairs, refs = refs[: 2 * n_faces], refs[2 * n_faces :]
    outs, (first, sent, held, table) = refs[:4], refs[4:]
    core = lax.axis_index("core")
    jumps = deck_jumps(masks, (f0, f1), (g0, g1))
    fields, corner = two_quarters(jumps, (high, low), corners, 0)
    first[...] = jumps[0]
    jumps = jumps + [third[...], fourth[...]]
    total = jnp.zeros((CASES, 1), F32)
    values = [quarter(part, i) + fields[i] for i in range(4)]
    for i in range(4):
        total = total + row_sum(jumps[i] * values[i])
    if n_faces == 1:
        corner_quarters = [quarter(corners, i) for i in range(4)]
        corner_quarters[2:] = by_span(*corner_quarters[2:])
        values[2:] = by_span(*values[2:])
        for i in range(4):
            outs[i][: CASES, :] = values[i]
            outs[i][CASES:, :] = corner_quarters[i]
    else:
        for i in range(4):
            outs[i][...] = values[i]
    sums = [
        row_sum(masks[0:1, :] * pairs[2 * k][...] * first[...] + masks[2:3, :] * pairs[2 * k + 1][...] * third[...])
        for k in range(n_faces)
    ]
    table[:, :NC] = corner_part[...] + corner
    lane = lax.broadcasted_iota(jnp.int32, (CASES, 128), 1)
    table[:, NC:] = column(lane, total, *sums)
    held[...] = table[pl.ds(pl.multiple_of(core * HALF, HALF), HALF), :]
    sent[...] = table[pl.ds(pl.multiple_of((1 - core) * HALF, HALF), HALF), :]


def total_of(got):
    part = got[0]
    for k in range(1, Z):
        part = part + got[k]
    return part


def first_coarse_kernel(got, coarse, out, scalars):
    part = total_of(got)
    total = part[:, :NC]
    load = SCALE * product(parts(total), parts(coarse[...]))
    curv = part[:, NC : NC + 1] + row_sum(load * total)
    rz = part[:, NC + 1 : NC + 2]
    lane = lax.broadcasted_iota(jnp.int32, (PIECE, 128), 1)
    row = jnp.concatenate([load, column(lane, rz / curv)], axis=1)
    for k in range(Y * X):
        out[k] = row
    scalars[...] = column(lane, rz, curv)


def second_coarse_kernel(got, coarse, scalars, out):
    part = total_of(got)
    total = part[:, :NC]
    load = SCALE * product(parts(total), parts(coarse[...]))
    own = part[:, NC : NC + 1] + row_sum(load * total)
    new = part[:, NC + 1 : NC + 2]
    cross = part[:, NC + 2 : NC + 3]
    rz, curv = scalars[:, 0:1], scalars[:, 1:2]
    ratio = new / rz
    second = new / (own + ratio * (2.0 * cross + ratio * curv))
    lane = lax.broadcasted_iota(jnp.int32, (PIECE, 128), 1)
    row = jnp.concatenate([second * load, column(lane, second, second * ratio)], axis=1)
    for k in range(Y * X):
        out[k] = row


def place_rows(mine, other, whole):
    core = lax.axis_index("core")
    whole[pl.ds(pl.multiple_of(core * HALF, HALF), HALF), :] = mine[...]
    whole[pl.ds(pl.multiple_of((1 - core) * HALF, HALF), HALF), :] = other[...]


def precond_kernel(masks, mine, other, f0, f1, f2, f3, g0, g1, g2, g3,
                   deck, joint, deck_behind, joint_behind, high, low,
                   v2, v3, u_high, u_low, image_deck, image_joint, res_deck, res_joint,
                   corner_deck, corner_joint, steps, whole):
    place_rows(mine, other, whole)
    load = parts(whole[:, :NC])
    step = whole[:, NC : NC + 1]
    steps[...] = whole[:, NC:]
    gaps = (deck, deck_behind, joint, joint_behind)
    under = slice(CASES, 2 * CASES)
    images = deck_jumps(masks, (f0, f1), (g0, g1)) + span_jumps(masks, (f2, f3), (g2, g3))
    corner = deck_jumps(masks, (f0, f1), (g0, g1), under) + span_jumps(masks, (f2, f3), (g2, g3), under)
    for i in range(4):
        image = images[i] + product(load, parts(corner[i]))
        gap = masks[i : i + 1, :] * gaps[i][...]
        res = (gap if i % 2 == 0 else -gap) - step * image
        if i == 0:
            corner_deck[...], image_deck[...], res_deck[...] = corner[i], image, res
        if i == 2:
            corner_joint[...], image_joint[...], res_joint[...] = corner[i], image, res
        keep(u_high, u_low, i, res)

    span_quarters(u_high, u_low, high, low, v2, v3)


def two_of(first, u_high, u_low, high, low):
    pair, rows = (u_high[...], u_low[...]), slice(0, IFACE)
    return [
        0.5 * product(pair, block_of((high, low), rows, slice(i * FACE, (i + 1) * FACE)))
        for i in (first, first + 1)
    ]


def span_quarters(u_high, u_low, high, low, v2, v3):
    v2[...], v3[...] = by_span(*two_of(2, u_high, u_low, high, low))


def deck_quarters(u_high, u_low, high, low, v0, v1):
    v0[...], v1[...] = two_of(0, u_high, u_low, high, low)


def final_kernel(masks, mine, other, steps, z_deck, z_joint, y_deck, y_joint,
                 image_deck, image_joint, res_deck, res_joint, corner_deck, corner_joint,
                 f0, f2, g0, g2, sol_deck, sol_joint, out_deck, out_joint, whole):
    place_rows(mine, other, whole)
    load = parts(whole[:, :NC])
    second, mixed = whole[:, NC : NC + 1], whole[:, NC + 1 : NC + 2]
    first = steps[:, 0:1] + mixed
    sol_deck[...] = first * z_deck[...] + second * y_deck[...]
    sol_joint[...] = first * z_joint[...] + second * y_joint[...]
    for i, res, field, ahead, image, corner, out in (
        (0, res_deck, f0, g0, image_deck, corner_deck, out_deck),
        (2, res_joint, f2, g2, image_joint, corner_joint, out_joint),
    ):
        reaction = masks[i : i + 1, :] * (field[...] - ahead[...])
        out[...] = (
            res[...] - second * reaction - mixed * image[...] - product(load, parts(corner[...]))
        )


def exchange(field):
    right, left, to_near, to_far = field
    right_got, left_got = cyclic(right, DECK, 1), cyclic(left, DECK, -1)
    return left_got, right_got, near(to_near), far(to_far)


def add_kernel(held, got, out):
    for k in range(Y * X):
        at = slice(k * PIECE, (k + 1) * PIECE)
        out[k] = held[at, :] + got[at, :]


def spread_kernel(got, out):
    part = got[0]
    for k in range(1, Y * X):
        part = part + got[k]
    for k in range(Z):
        out[k] = part


def scatter_rows(sent, held):
    (block,) = call(add_kernel, [(Y * X, PIECE, WIDE)], 2, "add")(held, swapped(sent))
    return lax.all_to_all(block, ("y", "x"), 0, 0)


def along_z(got):
    (copies,) = call(spread_kernel, [(Z, PIECE, WIDE)], 1, "spread")(got)
    return lax.all_to_all(copies, "z", 0, 0)


def gather_rows(copies):
    mine = lax.all_to_all(copies, ("y", "x"), 0, 0).reshape(HALF, WIDE)
    return mine, swapped(mine)


def after(values, *others):
    return lax.optimization_barrier((values, others))[0]


def local(flex, precond, corner_map, coarse_inverse, gap_deck, gap_joint, active):
    flex, precond, corners = flex[0, 0], precond[0, 0], corner_map[0, 0]
    deck, joint, active = gap_deck[0, 0], gap_joint[0, 0], active[0, 0]
    face, pair, field, stacked = (CASES, FACE), [(CASES, FACE)] * 2, [(CASES, FACE)] * 4, [(2 * CASES, FACE)] * 4
    wide, half, copies = (CASES, IFACE), (HALF, WIDE), (Y * X, PIECE, WIDE)
    narrow = [jax.ShapeDtypeStruct(wide, BF16)] * 2
    whole = pltpu.VMEM((CASES, WIDE), F32)

    def flexed(n_faces, v, name, shapes, *pairs):
        got = exchange(v)
        part, corner, third, fourth = call(
            flex_span_kernel, [wide, (CASES, NC), face, face], 8, name + "_span",
            estimate=cost(CASES // 2), grant=10,
        )(masks, *v[2:], *got[2:], *flex_pair, corners)
        *w, first, sent, held = call(
            functools.partial(flex_kernel, n_faces), shapes + [face, half, half], 12 + 2 * n_faces,
            name, scratch=(whole,), estimate=cost(CASES // 2), grant=10,
        )(masks, *v[:2], *got[:2], part, corner, third, fourth, *flex_pair, corners, *pairs)
        return *w, first, third, sent, held

    joint_behind = cyclic(joint, SPAN, 1)
    (lives,) = call(lives_kernel, [(8, FACE)], 1, "lives", smem=(0,), estimate=cost(4 * CASES))(active)
    deck_behind = cyclic(after(deck, lives), DECK, 1)
    lives_behind = cyclic(lives, SPAN, 1)
    gaps = (deck, joint, deck_behind, joint_behind)
    halves = [jax.ShapeDtypeStruct((IFACE, IFACE), BF16)] * 2
    pre_pair, flex_pair = (
        call(split_kernel, halves, 1, name, estimate=cost(CASES // 4), grant=4)(matrix)
        for matrix, name in ((precond, "split_precond"), (flex, "split_flex"))
    )
    (part,) = call(
        own_kernel, [wide], 5, "own", estimate=cost(CASES // 2), grant=10
    )(lives, deck, joint, *pre_pair)
    fourth = call(
        fourth_kernel, [jax.ShapeDtypeStruct(face, BF16)] * 2, 2, "fourth", estimate=cost(CASES // 8)
    )(joint_behind, lives_behind)
    behind = (*fourth, deck_behind, lives, lives_behind, part, *pre_pair)
    v2, v3, masks = call(
        functools.partial(behind_kernel, (2, 3)), pair + [(8, FACE)], 8, "behind_span",
        estimate=cost(CASES // 4), grant=10,
    )(*behind)
    v0, v1 = call(
        functools.partial(behind_kernel, (0, 1)), pair, 8, "behind_deck",
        estimate=cost(CASES // 4), grant=10,
    )(*behind)
    *w, z_deck, z_joint, sent, held = flexed(1, (v0, v1, v2, v3), "flex_first", stacked, deck, joint)
    rows = scatter_rows(sent, held)
    loads, scalars = call(first_coarse_kernel, [copies, (PIECE, 128)], 2, "coarse_first")(
        along_z(rows), coarse_inverse
    )
    got = exchange(after(w, rows))
    loads = after(loads, got)
    v2, v3, *u, image_deck, image_joint, res_deck, res_joint, corner_deck, corner_joint, steps = call(
        precond_kernel, pair + narrow + [face] * 6 + [(CASES, 128)], 17, "precond_span",
        scratch=(whole,), estimate=cost(CASES // 2), grant=10,
    )(masks, *gather_rows(loads), *w, *got, *gaps, *pre_pair)
    v0, v1 = call(
        deck_quarters, pair, 4, "precond_deck", estimate=cost(CASES // 2), grant=10
    )(*u, *pre_pair)
    *w, y_deck, y_joint, sent, held = flexed(
        2, (v0, v1, v2, v3), "flex_second", field, res_deck, res_joint, image_deck, image_joint
    )
    rows = scatter_rows(sent, held)
    left, behind = after((w[1], w[3]), rows)
    got = cyclic(left, DECK, -1), cyclic(behind, SPAN, -1)
    (loads,) = call(second_coarse_kernel, [copies], 3, "coarse_second")(
        along_z(rows), coarse_inverse, scalars
    )
    loads = after(loads, got)
    outs = call(
        final_kernel, [face] * 4, 18, "final", scratch=(whole,), grant=6
    )(
        masks, *gather_rows(loads), steps, z_deck, z_joint, y_deck, y_joint,
        image_deck, image_joint, res_deck, res_joint, corner_deck, corner_joint, w[0], w[2], *got,
    )
    return tuple(out[None, None] for out in outs)


def solution(mesh):
    mesh = Mesh(mesh.devices.reshape(Z, Y, X, 2), SPAN + DECK)
    block = P(SPAN, DECK, None, None)
    in_specs = (block, block, block, P(), block, block, P(SPAN, DECK, None))
    return jax.shard_map(
        local, mesh=mesh, in_specs=in_specs, out_specs=(block,) * 4, check_vma=False
    )
```

```python
import functools
import math

import jax
import jax.numpy as jnp
from jax import lax
from jax.experimental import pallas as pl
from jax.experimental.pallas import tpu as pltpu
from jax.sharding import Mesh
from jax.sharding import PartitionSpec as P

SPAN, DECK = ("z", "y"), ("x", "core")
SPANS, DECKS, Y, X, Z = 32, 8, 4, 4, 8
CASES, FACE, IFACE, NC, GB = 256, 256, 1024, 256, 4
WIDE = NC + 128
HALF = CASES // 2
PIECE = HALF // (Y * X)
SCALE = 1.0 / math.sqrt(SPANS * DECKS)
F32, BF16 = jnp.float32, jnp.bfloat16
VMEM = pl.BlockSpec(memory_space=pltpu.VMEM)
SMEM = pl.BlockSpec(memory_space=pltpu.SMEM)


def cyclic(block, axes, k):
    n = SPANS if axes == SPAN else DECKS
    return lax.ppermute(block, axes, [(i, (i + k) % n) for i in range(n)])


def near(block):
    return lax.ppermute(block, SPAN, [(i, i ^ 1) for i in range(SPANS)])


def far(block):
    return lax.ppermute(block, SPAN, [(i, (i + (1 if i % 2 else -1)) % SPANS) for i in range(SPANS)])


def swapped(block):
    return lax.ppermute(block, "core", [(0, 1), (1, 0)])


def parts(value):
    high = value.astype(BF16)
    return high, (value - high.astype(F32)).astype(BF16)


def product(left, right, dims=(((1,), (0,)), ((), ()))):
    dot = functools.partial(lax.dot_general, dimension_numbers=dims, preferred_element_type=F32)
    return dot(left[0], right[0]) + (dot(left[0], right[1]) + dot(left[1], right[0]))


TRANS = (((1,), (1,)), ((), ()))


def quarter(ref, i):
    return ref[:, i * FACE : (i + 1) * FACE]


def column(lane, *values):
    out = jnp.zeros((values[0].shape[0], 128), F32)
    for i, value in enumerate(values):
        out = jnp.where(lane == i, value, out)
    return out


def row_sum(value):
    return jnp.sum(value, axis=1, keepdims=True)


def cost(rows):
    return pl.CostEstimate(flops=6 * rows * IFACE * IFACE, bytes_accessed=8 << 20, transcendentals=0)


def call(body, outs, n_in, name, smem=(), scratch=(), estimate=None, grant=2):
    return pl.pallas_call(
        body,
        out_shape=tuple(s if isinstance(s, jax.ShapeDtypeStruct) else jax.ShapeDtypeStruct(s, F32) for s in outs),
        in_specs=[SMEM if i in smem else VMEM for i in range(n_in)],
        out_specs=tuple(VMEM for _ in outs),
        scratch_shapes=list(scratch),
        compiler_params=pltpu.CompilerParams(vmem_limit_bytes=grant << 20),
        cost_estimate=estimate,
        name=name,
    )


def keep(u_high, u_low, i, value):
    high, low = parts(value)
    u_high[:, i * FACE : (i + 1) * FACE] = high
    u_low[:, i * FACE : (i + 1) * FACE] = low


def position():
    span = lax.axis_index("z") * Y + lax.axis_index("y")
    return span, lax.axis_index("x") * 2 + lax.axis_index("core")


def live_row(ref, on):
    block = lax.broadcasted_iota(jnp.int32, (1, FACE), 1) // (FACE // GB)
    row = jnp.zeros((1, FACE), F32)
    for b in range(GB):
        row = jnp.where(block == b, ref[b].astype(F32), row)
    return row * on.astype(F32)


def block_of(pair, rows, columns):
    return pair[0][rows, columns], pair[1][rows, columns]


def faces_times(first, third, matrix, row, i):
    at = slice(i * FACE, (i + 1) * FACE)
    return product(first, block_of(matrix, slice(row, row + FACE), at)) + product(
        third, block_of(matrix, slice(row + 2 * FACE, row + 3 * FACE), at)
    )


def split_kernel(matrix, high, low):
    for i in range(4):
        keep(high, low, i, quarter(matrix, i))


def fourth_kernel(joint_behind, lives_behind, high, low):
    high[...], low[...] = parts(lives_behind[0:1, :] * joint_behind[...])


def by_span(near_value, far_value):
    odd = lax.rem(position()[0], 2) == 1
    return jnp.where(odd, far_value, near_value), jnp.where(odd, near_value, far_value)


def lives_kernel(active, out):
    out[...] = jnp.broadcast_to(live_row(active, position()[0] < SPANS - 1), (8, FACE))


def own_kernel(lives, deck, joint, high, low, part):
    first = parts((position()[1] < DECKS - 1).astype(F32) * deck[...])
    third = parts(lives[0:1, :] * joint[...])
    for i in range(4):
        part[:, i * FACE : (i + 1) * FACE] = faces_times(first, third, (high, low), 0, i)


def behind_kernel(which, joint_high, joint_low, deck_behind, lives, lives_behind, part, high, low, *outs):
    _, across = position()
    ones = jnp.ones((1, FACE), F32)
    lives = (
        ones * (across < DECKS - 1).astype(F32),
        ones * (across > 0).astype(F32),
        lives[0:1, :],
        lives_behind[0:1, :],
    )
    if len(outs) == 3:
        outs[2][...] = jnp.concatenate(lives + (jnp.zeros((4, FACE), F32),), axis=0)
    second, fourth = parts(lives[1] * deck_behind[...]), (joint_high[...], joint_low[...])
    values = [0.5 * (quarter(part, i) - faces_times(second, fourth, (high, low), FACE, i)) for i in which]
    if which[0] == 2:
        values = by_span(*values)
    outs[0][...], outs[1][...] = values


def deck_jumps(masks, own, got, rows=slice(0, CASES)):
    return [masks[i : i + 1, :] * (own[i][rows, :] - got[i][rows, :]) for i in range(2)]


def span_jumps(masks, own, got, rows=slice(0, CASES)):
    ahead, behind = by_span(own[0][rows, :] - got[0][rows, :], own[1][rows, :] - got[1][rows, :])
    return [masks[2:3, :] * ahead, masks[3:4, :] * behind]


def two_quarters(jumps, matrix, corners, at):
    pair = parts(jnp.concatenate(jumps, axis=1))
    rows = slice(at, at + 2 * FACE)
    fields = [product(pair, block_of(matrix, rows, slice(i * FACE, (i + 1) * FACE))) for i in range(4)]
    return fields, product(pair, parts(corners[:, rows]), TRANS)


def flex_span_kernel(masks, f3, f2, g3, g2, high, low, corners, part, corner_part, third, fourth):
    third[...], fourth[...] = span_jumps(masks, (f2, f3), (g2, g3))
    fields, corner = two_quarters([third[...], fourth[...]], (high, low), corners, 2 * FACE)
    for i in range(4):
        part[:, i * FACE : (i + 1) * FACE] = fields[i]
    corner_part[...] = corner


def flex_kernel(n_faces, masks, f0, f1, g0, g1, part, corner_part, third, fourth, high, low, corners, *refs):
    pairs, refs = refs[: 2 * n_faces], refs[2 * n_faces :]
    outs, (first, sent, held, table) = refs[:4], refs[4:]
    core = lax.axis_index("core")
    jumps = deck_jumps(masks, (f0, f1), (g0, g1))
    fields, corner = two_quarters(jumps, (high, low), corners, 0)
    first[...] = jumps[0]
    jumps = jumps + [third[...], fourth[...]]
    total = jnp.zeros((CASES, 1), F32)
    values = [quarter(part, i) + fields[i] for i in range(4)]
    for i in range(4):
        total = total + row_sum(jumps[i] * values[i])
    if n_faces == 1:
        corner_quarters = [quarter(corners, i) for i in range(4)]
        corner_quarters[2:] = by_span(*corner_quarters[2:])
        values[2:] = by_span(*values[2:])
        for i in range(4):
            outs[i][: CASES, :] = values[i]
            outs[i][CASES:, :] = corner_quarters[i]
    else:
        for i in range(4):
            outs[i][...] = values[i]
    sums = [
        row_sum(masks[0:1, :] * pairs[2 * k][...] * first[...] + masks[2:3, :] * pairs[2 * k + 1][...] * third[...])
        for k in range(n_faces)
    ]
    table[:, :NC] = corner_part[...] + corner
    lane = lax.broadcasted_iota(jnp.int32, (CASES, 128), 1)
    table[:, NC:] = column(lane, total, *sums)
    held[...] = table[pl.ds(pl.multiple_of(core * HALF, HALF), HALF), :]
    sent[...] = table[pl.ds(pl.multiple_of((1 - core) * HALF, HALF), HALF), :]


def total_of(got):
    part = got[0]
    for k in range(1, Z):
        part = part + got[k]
    return part


def first_coarse_kernel(got, coarse, out, scalars):
    part = total_of(got)
    total = part[:, :NC]
    load = SCALE * product(parts(total), parts(coarse[...]))
    curv = part[:, NC : NC + 1] + row_sum(load * total)
    rz = part[:, NC + 1 : NC + 2]
    lane = lax.broadcasted_iota(jnp.int32, (PIECE, 128), 1)
    row = jnp.concatenate([load, column(lane, rz / curv)], axis=1)
    for k in range(Y * X):
        out[k] = row
    scalars[...] = column(lane, rz, curv)


def second_coarse_kernel(got, coarse, scalars, out):
    part = total_of(got)
    total = part[:, :NC]
    load = SCALE * product(parts(total), parts(coarse[...]))
    own = part[:, NC : NC + 1] + row_sum(load * total)
    new = part[:, NC + 1 : NC + 2]
    cross = part[:, NC + 2 : NC + 3]
    rz, curv = scalars[:, 0:1], scalars[:, 1:2]
    ratio = new / rz
    second = new / (own + ratio * (2.0 * cross + ratio * curv))
    lane = lax.broadcasted_iota(jnp.int32, (PIECE, 128), 1)
    row = jnp.concatenate([second * load, column(lane, second, second * ratio)], axis=1)
    for k in range(Y * X):
        out[k] = row


def place_rows(mine, other, whole):
    core = lax.axis_index("core")
    whole[pl.ds(pl.multiple_of(core * HALF, HALF), HALF), :] = mine[...]
    whole[pl.ds(pl.multiple_of((1 - core) * HALF, HALF), HALF), :] = other[...]


def precond_kernel(masks, mine, other, f0, f1, f2, f3, g0, g1, g2, g3,
                   deck, joint, deck_behind, joint_behind, high, low,
                   v2, v3, u_high, u_low, image_deck, image_joint, res_deck, res_joint,
                   corner_deck, corner_joint, steps, whole):
    place_rows(mine, other, whole)
    load = parts(whole[:, :NC])
    step = whole[:, NC : NC + 1]
    steps[...] = whole[:, NC:]
    gaps = (deck, deck_behind, joint, joint_behind)
    under = slice(CASES, 2 * CASES)
    images = deck_jumps(masks, (f0, f1), (g0, g1)) + span_jumps(masks, (f2, f3), (g2, g3))
    corner = deck_jumps(masks, (f0, f1), (g0, g1), under) + span_jumps(masks, (f2, f3), (g2, g3), under)
    for i in range(4):
        image = images[i] + product(load, parts(corner[i]))
        gap = masks[i : i + 1, :] * gaps[i][...]
        res = (gap if i % 2 == 0 else -gap) - step * image
        if i == 0:
            corner_deck[...], image_deck[...], res_deck[...] = corner[i], image, res
        if i == 2:
            corner_joint[...], image_joint[...], res_joint[...] = corner[i], image, res
        keep(u_high, u_low, i, res)

    span_quarters(u_high, u_low, high, low, v2, v3)


def two_of(first, u_high, u_low, high, low):
    pair, rows = (u_high[...], u_low[...]), slice(0, IFACE)
    return [
        0.5 * product(pair, block_of((high, low), rows, slice(i * FACE, (i + 1) * FACE)))
        for i in (first, first + 1)
    ]


def span_quarters(u_high, u_low, high, low, v2, v3):
    v2[...], v3[...] = by_span(*two_of(2, u_high, u_low, high, low))


def deck_quarters(u_high, u_low, high, low, v0, v1):
    v0[...], v1[...] = two_of(0, u_high, u_low, high, low)


def final_kernel(masks, mine, other, steps, z_deck, z_joint, y_deck, y_joint,
                 image_deck, image_joint, res_deck, res_joint, corner_deck, corner_joint,
                 f0, f2, g0, g2, sol_deck, sol_joint, out_deck, out_joint, whole):
    place_rows(mine, other, whole)
    load = parts(whole[:, :NC])
    second, mixed = whole[:, NC : NC + 1], whole[:, NC + 1 : NC + 2]
    first = steps[:, 0:1] + mixed
    sol_deck[...] = first * z_deck[...] + second * y_deck[...]
    sol_joint[...] = first * z_joint[...] + second * y_joint[...]
    for i, res, field, ahead, image, corner, out in (
        (0, res_deck, f0, g0, image_deck, corner_deck, out_deck),
        (2, res_joint, f2, g2, image_joint, corner_joint, out_joint),
    ):
        reaction = masks[i : i + 1, :] * (field[...] - ahead[...])
        out[...] = (
            res[...] - second * reaction - mixed * image[...] - product(load, parts(corner[...]))
        )


def exchange(field):
    right, left, to_near, to_far = field
    right_got, left_got = cyclic(right, DECK, 1), cyclic(left, DECK, -1)
    far_got = far(to_far)
    return left_got, right_got, near(to_near), far_got


def add_kernel(held, got, out):
    for k in range(Y * X):
        at = slice(k * PIECE, (k + 1) * PIECE)
        out[k] = held[at, :] + got[at, :]


def spread_kernel(got, out):
    part = got[0]
    for k in range(1, Y * X):
        part = part + got[k]
    for k in range(Z):
        out[k] = part


def scatter_rows(sent, held):
    (block,) = call(add_kernel, [(Y * X, PIECE, WIDE)], 2, "add")(held, swapped(sent))
    return lax.all_to_all(block, ("y", "x"), 0, 0)


def along_z(got):
    (copies,) = call(spread_kernel, [(Z, PIECE, WIDE)], 1, "spread")(got)
    return lax.all_to_all(copies, "z", 0, 0)


def gather_rows(copies):
    mine = lax.all_to_all(copies, ("y", "x"), 0, 0).reshape(HALF, WIDE)
    return mine, swapped(mine)


def after(values, *others):
    return lax.optimization_barrier((values, others))[0]


def local(flex, precond, corner_map, coarse_inverse, gap_deck, gap_joint, active):
    flex, precond, corners = flex[0, 0], precond[0, 0], corner_map[0, 0]
    deck, joint, active = gap_deck[0, 0], gap_joint[0, 0], active[0, 0]
    face, pair, field, stacked = (CASES, FACE), [(CASES, FACE)] * 2, [(CASES, FACE)] * 4, [(2 * CASES, FACE)] * 4
    wide, half, copies = (CASES, IFACE), (HALF, WIDE), (Y * X, PIECE, WIDE)
    narrow = [jax.ShapeDtypeStruct(wide, BF16)] * 2
    whole = pltpu.VMEM((CASES, WIDE), F32)

    def flexed(n_faces, v, name, shapes, *pairs):
        got = exchange(v)
        part, corner, third, fourth = call(
            flex_span_kernel, [wide, (CASES, NC), face, face], 8, name + "_span",
            estimate=cost(CASES // 2), grant=10,
        )(masks, *v[:1:-1], *got[:1:-1], *flex_pair, corners)
        *w, first, sent, held = call(
            functools.partial(flex_kernel, n_faces), shapes + [face, half, half], 12 + 2 * n_faces,
            name, scratch=(whole,), estimate=cost(CASES // 2), grant=10,
        )(masks, *v[:2], *got[:2], part, corner, third, fourth, *flex_pair, corners, *pairs)
        return *w, first, third, sent, held

    joint_behind = cyclic(joint, SPAN, 1)
    (lives,) = call(lives_kernel, [(8, FACE)], 1, "lives", smem=(0,), estimate=cost(4 * CASES))(active)
    deck_behind = cyclic(after(deck, lives), DECK, 1)
    lives_behind = cyclic(lives, SPAN, 1)
    gaps = (deck, joint, deck_behind, joint_behind)
    halves = [jax.ShapeDtypeStruct((IFACE, IFACE), BF16)] * 2
    pre_pair, flex_pair = (
        call(split_kernel, halves, 1, name, estimate=cost(CASES // 4), grant=4)(matrix)
        for matrix, name in ((precond, "split_precond"), (flex, "split_flex"))
    )
    (part,) = call(
        own_kernel, [wide], 5, "own", estimate=cost(CASES // 2), grant=10
    )(lives, deck, joint, *pre_pair)
    fourth = call(
        fourth_kernel, [jax.ShapeDtypeStruct(face, BF16)] * 2, 2, "fourth", estimate=cost(CASES // 8)
    )(joint_behind, lives_behind)
    behind = (*fourth, deck_behind, lives, lives_behind, part, *pre_pair)
    v2, v3, masks = call(
        functools.partial(behind_kernel, (2, 3)), pair + [(8, FACE)], 8, "behind_span",
        estimate=cost(CASES // 4), grant=10,
    )(*behind)
    v0, v1 = call(
        functools.partial(behind_kernel, (0, 1)), pair, 8, "behind_deck",
        estimate=cost(CASES // 4), grant=10,
    )(*behind)
    *w, z_deck, z_joint, sent, held = flexed(1, (v0, v1, v2, v3), "flex_first", stacked, deck, joint)
    rows = scatter_rows(sent, held)
    loads, scalars = call(first_coarse_kernel, [copies, (PIECE, 128)], 2, "coarse_first")(
        along_z(rows), coarse_inverse
    )
    got = exchange(after(w, rows))
    loads = after(loads, got)
    v2, v3, *u, image_deck, image_joint, res_deck, res_joint, corner_deck, corner_joint, steps = call(
        precond_kernel, pair + narrow + [face] * 6 + [(CASES, 128)], 17, "precond_span",
        scratch=(whole,), estimate=cost(CASES // 2), grant=10,
    )(masks, *gather_rows(loads), *w, *got, *gaps, *pre_pair)
    v0, v1 = call(
        deck_quarters, pair, 4, "precond_deck", estimate=cost(CASES // 2), grant=10
    )(*u, *pre_pair)
    *w, y_deck, y_joint, sent, held = flexed(
        2, (v0, v1, v2, v3), "flex_second", field, res_deck, res_joint, image_deck, image_joint
    )
    rows = scatter_rows(sent, held)
    left, behind = after((w[1], w[3]), rows)
    got = cyclic(left, DECK, -1), cyclic(behind, SPAN, -1)
    (loads,) = call(second_coarse_kernel, [copies], 3, "coarse_second")(
        along_z(rows), coarse_inverse, scalars
    )
    loads = after(loads, got)
    outs = call(
        final_kernel, [face] * 4, 18, "final", scratch=(whole,), grant=6
    )(
        masks, *gather_rows(loads), steps, z_deck, z_joint, y_deck, y_joint,
        image_deck, image_joint, res_deck, res_joint, corner_deck, corner_joint, w[0], w[2], *got,
    )
    return tuple(out[None, None] for out in outs)


def solution(mesh):
    mesh = Mesh(mesh.devices.reshape(Z, Y, X, 2), SPAN + DECK)
    block = P(SPAN, DECK, None, None)
    in_specs = (block, block, block, P(), block, block, P(SPAN, DECK, None))
    return jax.shard_map(
        local, mesh=mesh, in_specs=in_specs, out_specs=(block,) * 4, check_vma=False
    )
```
